512 devices in a mesh: seq: 128 (over y, z, core), win: 4 (over x).
Axes of the slice: x: 4, y: 8, z: 8, core: 2. Of those that a mesh axis runs over, the one named last changes fastest.
Arguments:
- queries: bfloat16 [65536, 1024], P(('win', 'seq')), parts along dimension 0, may hold values from -6 to 6
- key_rows: bfloat16 [65536, 1024], P(('win', 'seq')), parts along dimension 0, may hold values from -6 to 6
- value_rows: bfloat16 [65536, 2048], P(('win', 'seq')), parts along dimension 0, may hold values from -6 to 6
- residual: bfloat16 [65536, 1024], P(('win', 'seq')), parts along dimension 0, may hold values from -6 to 6
- out_weight: bfloat16 [2048, 1024], P(None, 'seq'), may hold values from -0.125 to 0.125
- expert_in: bfloat16 [128, 1024, 768], P('seq'), may hold values from -0.1875 to 0.1875
- expert_out: bfloat16 [128, 384, 1024], P('seq'), may hold values from -0.3125 to 0.3125
- expert_ids: int32 [65536, 2], P(('win', 'seq')), parts along dimension 0, may hold values from 0 to 127, all different within a row; in each aligned block of 128 rows (0 to 127, 128 to 255, ...) at most 4 rows name the same one
- gate_values: float32 [65536, 2], P(('win', 'seq')), parts along dimension 0, may hold values from 0.2 to 1
Outputs:
- layer_out: bfloat16 [65536, 1024], P(('win', 'seq')), parts along dimension 0
The draws below stay inside these ranges and needn't reach their ends.
There are 4 independent parts, one for each index of `win`. The reference program is written for one: setup_inputs(seed, part) draws one part's arguments, and reference() takes and returns one part's arrays. A program takes and returns all parts, laid end to end along the dimension named above; an argument that names none is the same for every part. Nothing has to cross between parts.
Inputs may be any that keep to these rules, and one draw needn't show every extreme that they name: `expert_ids`: the 2 ids of a row differ. Within the rows of one block of 128 tokens no expert is named by more than 4 rows, a bound that some block reaches. Every expert is named somewhere.
All inputs are finite; a program needn't handle non-finite values.
Results may differ from the reference program's by a relative error of at most 0.013.
Values may be sent and summed in bfloat16 or wider, within the bound.
A program may use at most 128 MiB of HBM per device.

```python
import math
import jax
import jax.numpy as jnp
import numpy as np
from jax import lax

D = 1024
H = 16
DK = 64
DV = 128
HE = 384
TOP = 2
TOK_DEV = 128
TOKENS = 16384
EXPERTS = 128
CAP = 4
N_SEQ = 128


def block_levels(key, dims, shards, low, top_value):
    gain, own = 1.0, jax.random.fold_in(key, 6)
    for dim, blocks in shards:
        draws = jnp.exp(jax.random.uniform(jax.random.fold_in(own, dim), (blocks,), jnp.float32, low / len(shards), top_value / len(shards)))
        gain = gain * jnp.repeat(draws, dims[dim] // blocks).reshape([-1 if axis == dim else 1 for axis in range(len(dims))])
    return gain


def deal_out(own_key, own, number, rows, amount, top, most, skew):
    ranking = jax.random.permutation(own_key, amount)
    packed, common = load_shares(amount, rows * top, most, skew, True), load_shares(amount, rows * top, most, skew, False)
    places = jnp.arange(amount)

    def named(tallies, turn):
        used = int((tallies > 0).sum())
        fixed = max(1, used // 4)
        moved = fixed + (places - fixed + turn * (used - fixed)) % max(1, amount - fixed)
        return jnp.zeros((amount,), jnp.int32).at[ranking[jnp.where(places < fixed, places, moved)]].set(jnp.asarray(tallies, jnp.int32))

    tallies = jnp.where(number % 4 == 0, named(packed, number // 4), named(common, number - number // 4 - 1))
    mixed = jax.random.permutation(jax.random.fold_in(own, 3), amount)
    giver, sink = mixed[0:amount // 2 * 2:2], mixed[1:amount // 2 * 2:2]
    slack = jnp.minimum(tallies[giver] - 1, most - tallies[sink]) // 2
    slack = jnp.where((giver == ranking[0]) | (sink == ranking[0]) | (tallies[sink] == 0), 0, jnp.maximum(slack, 0))
    moved = jax.random.randint(jax.random.fold_in(own, 4), (amount // 2,), 0, 1 << 20) % (slack + 1)
    tallies = tallies.at[giver].add(-moved).at[sink].add(moved)
    labels = jnp.searchsorted(jnp.cumsum(tallies), jnp.arange(rows * top), side="right").astype(jnp.int32)
    grid = labels.reshape(top, rows).T
    grid = grid[jax.random.permutation(jax.random.fold_in(own, 1), rows)]
    turn = jax.random.randint(jax.random.fold_in(own, 2), (rows, 1), 0, top)
    return jnp.take_along_axis(grid, (jnp.arange(top)[None, :] + turn) % top, axis=1)


def load_shares(count, total, bound, skew, full):
    portions = [(1 << 20) // math.isqrt(rank ** skew) + 1 for rank in range(1, count + 1)]
    largest = bound if full else min(bound, max(-(-total // count), total * portions[0] // sum(portions)))
    least = 1 if total - largest >= count - 1 else 0
    counts, spare = [largest] + [least] * (count - 1), total - largest - least * (count - 1)
    while spare > 0:
        candidates = [i for i in range(1, count) if counts[i] < largest] or [i for i in range(1, count) if counts[i] < bound]
        mass, left = sum([portions[i] for i in candidates]), spare
        for i in candidates:
            extra = min(bound - counts[i], max(1, left * portions[i] // mass), spare)
            counts[i] = counts[i] + extra
            spare = spare - extra
    return np.array(counts)


def bell_draw(key, extent, width, most, pieces=(), held_as=jnp.bfloat16):
    drawn = jax.random.normal(key, extent, jnp.float32) * width
    if len(pieces) > 0:
        drawn = block_levels(key, extent, pieces, -0.22, 0.18) * drawn
    return jnp.clip(drawn, min=-most, max=most).astype(held_as)


def setup_inputs(seed: int = 0, part: int = 0) -> dict:
    splits = jax.random.split(jax.random.key(seed), 10)
    part_splits = jax.random.split(jax.random.fold_in(splits[9], part), 10)
    queries = bell_draw(part_splits[0], (TOKENS, H * DK), 1.0, 6.0, ((0, 128),))
    key_rows = bell_draw(part_splits[1], (TOKENS, H * DK), 1.0, 6.0, ((0, 128),))
    value_rows = bell_draw(part_splits[2], (TOKENS, H * DV), 1.0, 6.0, ((0, 128),))
    residual = bell_draw(part_splits[3], (TOKENS, D), 1.0, 6.0, ((0, 128),))
    out_weight = bell_draw(splits[4], (H * DV, D), (H * DV) ** -0.5, 0.125, ((1, 128),))
    expert_in = bell_draw(splits[5], (EXPERTS, D, 2 * HE), D ** -0.5, 0.1875, ((0, 128),))
    expert_out = bell_draw(splits[6], (EXPERTS, HE, D), HE ** -0.5, 0.3125, ((0, 128),))
    expert_ids_keys = jax.random.split(jax.random.fold_in(part_splits[7], 1), TOKENS // TOK_DEV)
    expert_ids_turns = jax.random.permutation(jax.random.fold_in(part_splits[7], 3), TOKENS // TOK_DEV)
    expert_ids = jax.vmap(lambda own, number: deal_out(jax.random.fold_in(part_splits[7], 2), own, number, TOK_DEV, EXPERTS, TOP, CAP, 2))(expert_ids_keys, expert_ids_turns).reshape((TOKENS, TOP))
    gate_values = jnp.clip(0.2 + 0.8 * jax.random.uniform(part_splits[8], (TOKENS, TOP), jnp.float32) ** block_levels(part_splits[8], (TOKENS, TOP), ((0, 128),), -0.2, 0.2), 0.2, 1.0)
    return dict(queries=queries, key_rows=key_rows, value_rows=value_rows, residual=residual, out_weight=out_weight, expert_in=expert_in, expert_out=expert_out, expert_ids=expert_ids, gate_values=gate_values)


def reference(queries, key_rows, value_rows, residual, out_weight, expert_in, expert_out, expert_ids, gate_values):
    q_blocks = queries.reshape(N_SEQ, TOK_DEV, H, DK)
    k_blocks = key_rows.reshape(N_SEQ, TOK_DEV, H, DK)
    v_blocks = value_rows.reshape(N_SEQ, TOK_DEV, H, DV)
    causal = jnp.arange(TOK_DEV)[:, None] >= jnp.arange(TOK_DEV)[None, :]
    starts = jnp.arange(N_SEQ).astype(jnp.float32) * TOK_DEV

    def block_step(carried, block_in):
        q_block, k_block, v_block, start_pos = block_in
        q_float = q_block.astype(jnp.float32)
        k_float = k_block.astype(jnp.float32)
        v_float = v_block.astype(jnp.float32)
        scores = jnp.einsum('thd,shd->hts', q_float, k_float)
        scores = jnp.where(causal[None], scores, 0.0).astype(jnp.bfloat16)
        scores = lax.optimization_barrier(scores).astype(jnp.float32)
        intra_sum = jnp.einsum('hts,she->the', scores, v_float)
        inter_sum = jnp.einsum('thd,hde->the', q_float, carried, precision=lax.Precision.HIGHEST)
        position = start_pos + jnp.arange(TOK_DEV).astype(jnp.float32)
        scaling = lax.rsqrt((position + 1.0) * DK)
        produced = ((intra_sum + inter_sum) * scaling[:, None, None]).astype(jnp.bfloat16)
        carried = carried + jnp.einsum('thd,the->hde', k_float, v_float)
        return (carried, produced)
    _, attended = lax.scan(block_step, jnp.zeros((H, DK, DV), jnp.float32), (q_blocks, k_blocks, v_blocks, starts))
    attended = attended.reshape(TOKENS, H * DV)
    projected = jnp.dot(attended, out_weight, preferred_element_type=jnp.float32)
    hidden = (residual.astype(jnp.float32) + projected).astype(jnp.bfloat16)
    hidden_float = hidden.astype(jnp.float32)
    normed = (hidden_float * lax.rsqrt(lax.optimization_barrier(jnp.mean(hidden_float * hidden_float, axis=-1, keepdims=True)) + 1e-06)).astype(jnp.bfloat16)
    ids_block = expert_ids.reshape(N_SEQ, TOK_DEV * TOP)
    one_hot = (ids_block[..., None] == jnp.arange(EXPERTS)[None, None, :]).astype(jnp.int32)
    earlier = jnp.cumsum(one_hot, axis=1) - one_hot
    slot_index = lax.optimization_barrier(jnp.sum(earlier * one_hot, axis=-1))
    block_of = jnp.arange(N_SEQ)[:, None].astype(jnp.int32)
    dest_row = (ids_block * (N_SEQ * CAP) + block_of * CAP + slot_index).reshape(-1).astype(jnp.int32)
    sources = jnp.repeat(normed, TOP, axis=0)
    buffer = jnp.zeros((EXPERTS * N_SEQ * CAP, D), jnp.bfloat16).at[dest_row].set(sources)
    buffer = buffer.reshape(EXPERTS, N_SEQ * CAP, D)

    def run_expert(item):
        rows_in, weight_in, weight_out = item
        act = jnp.dot(rows_in, weight_in, preferred_element_type=jnp.float32)
        inner = (jax.nn.silu(act[:, :HE]) * act[:, HE:]).astype(jnp.bfloat16)
        return jnp.dot(inner, weight_out, preferred_element_type=jnp.float32).astype(jnp.bfloat16)
    expert_rows = lax.map(run_expert, (buffer, expert_in, expert_out))
    picked = expert_rows.reshape(EXPERTS * N_SEQ * CAP, D)[dest_row]
    combined = lax.optimization_barrier(jnp.sum(picked.astype(jnp.float32).reshape(TOKENS, TOP, D) * gate_values[:, :, None], axis=1))
    return (hidden_float + combined).astype(jnp.bfloat16)
```

```python
import functools

import jax
import jax.numpy as jnp
from jax import lax
from jax.experimental import pallas as pl
from jax.experimental.pallas import tpu as pltpu
from jax.sharding import PartitionSpec as P

TOP = 2
CAP = 4
GROUPS = 4
MESH = pl.DeviceIdType.MESH
BF = jnp.bfloat16
F32 = jnp.float32


def dot(a, b, dims=((1,), (0,))):
    return lax.dot_general(a, b, (dims, ((), ())), preferred_element_type=F32)


def layer_kernel(
    ny,
    nz,
    heads,
    dk,
    dv,
    q_ref,
    k_ref,
    v_ref,
    res_ref,
    wt_ref,
    win_hbm,
    wout_hbm,
    ids_ref,
    gates_ref,
    o_ref,
    s_loc,
    tot,
    p_out,
    r1,
    r2,
    r3,
    w_loc,
    w_all,
    intra,
    attended,
    win,
    wout,
    xb,
    xr,
    yb,
    ret,
    s1_send,
    s1_recv,
    s2_send,
    s2_recv,
    s3_send,
    s3_recv,
    w1_send,
    w1_recv,
    ring_send,
    ring_recv,
    sib_send,
    sib_recv,
    x_send,
    x_recv,
    y_send,
    y_recv,
    win_sem,
):
    n = ny * nz * 2
    row = nz * 2
    length = q_ref.shape[0]
    width = res_ref.shape[1]
    he = wout.shape[0]
    quarter = w_loc.shape[2]
    me = lax.axis_index("seq")
    y, z, c = me // row, lax.rem(me // 2, nz), lax.rem(me, 2)
    at_row = lax.rem(me, row)

    def seq(yy, zz, cc):
        return yy * row + zz * 2 + cc

    def remote(src, dst, ssem, rsem, dev):
        return pltpu.make_async_remote_copy(
            src_ref=src,
            dst_ref=dst,
            send_sem=ssem,
            recv_sem=rsem,
            device_id={"seq": dev},
            device_id_type=MESH,
        )

    def drain(ref, sem):
        pltpu.make_async_copy(ref, ref, sem).wait()

    barrier = pltpu.get_barrier_semaphore()

    def greet(i, _):
        pl.semaphore_signal(
            barrier, inc=1, device_id={"seq": lax.rem(me + i, n)}, device_id_type=MESH
        )
        return 0

    lax.fori_loop(1, n, greet, 0)

    load_in = pltpu.make_async_copy(win_hbm, win, win_sem.at[0])
    load_out = pltpu.make_async_copy(wout_hbm, wout, win_sem.at[1])
    load_in.start()
    load_out.start()

    def states(p, _):
        kp = k_ref[:, pl.ds(pl.multiple_of(p * 2 * dk, 2 * dk), 2 * dk)]
        vp = v_ref[:, pl.ds(pl.multiple_of(p * 2 * dv, 2 * dv), 2 * dv)]
        kv = dot(kp, vp, ((0,), (0,)))
        s_loc[2 * p] = kv[:dk, :dv].astype(BF)
        s_loc[2 * p + 1] = kv[dk:, dv:].astype(BF)
        return 0

    lax.fori_loop(0, heads // 2, states, 0)
    for part in range(4):
        w_loc[part] = wt_ref[:, part * quarter : (part + 1) * quarter]

    pl.semaphore_wait(barrier, n - 1)

    pltpu.make_async_copy(s_loc.at[at_row], r1.at[at_row], s1_recv).start()

    def phase1(i, _):
        to = lax.rem(at_row + i, row)
        remote(s_loc.at[to], r1.at[at_row], s1_send, s1_recv, y * row + to).start()
        return 0

    lax.fori_loop(1, row, phase1, 0)

    def own_part(part, which):
        pltpu.make_async_copy(
            w_loc.at[part], w_all.at[part, y, z, c], w1_recv.at[which]
        ).start()

    own_part(2 * c, 0)
    own_part(2 * c + 1, 1)

    def along_z(i, _):
        to = lax.rem(at_row + i, row)
        part = 2 * lax.rem(to, 2)
        remote(
            w_loc.at[part], w_all.at[part, y, z, c], w1_send, w1_recv.at[0], y * row + to
        ).start()
        return 0

    def along_y(i, _):
        cc = lax.rem(c + i, 2)
        yy = lax.rem(y + i // 2, ny)
        part = 2 * cc + 1
        remote(
            w_loc.at[part], w_all.at[part, y, z, c], w1_send, w1_recv.at[1], seq(yy, z, cc)
        ).start()
        return 0

    lax.fori_loop(1, row, along_z, 0)
    lax.fori_loop(1, 2 * ny, along_y, 0)

    t_row = lax.broadcasted_iota(jnp.int32, (2 * length, length), 0)
    t_col = lax.broadcasted_iota(jnp.int32, (2 * length, length), 1)
    causal = lax.rem(t_row, length) >= t_col
    first = lax.broadcasted_iota(jnp.int32, (length, 2 * dk), 1) < dk

    def two_heads(p):
        qp = q_ref[:, pl.ds(pl.multiple_of(p * 2 * dk, 2 * dk), 2 * dk)]
        zero = jnp.zeros_like(qp)
        return jnp.concatenate(
            [jnp.where(first, qp, zero), jnp.where(first, zero, qp)], axis=0
        )

    def inside(p, _):
        kp = k_ref[:, pl.ds(pl.multiple_of(p * 2 * dk, 2 * dk), 2 * dk)]
        at = pl.multiple_of(p * 2 * dv, 2 * dv)
        scores = dot(two_heads(p), kp, ((1,), (1,)))
        scores = jnp.where(causal, scores, 0.0).astype(BF)
        vp = v_ref[:, pl.ds(at, 2 * dv)]
        intra[:, pl.ds(at, dv)] = dot(scores[:length], vp[:, :dv])
        intra[:, pl.ds(pl.multiple_of(at + dv, dv), dv)] = dot(scores[length:], vp[:, dv:])
        return 0

    half = heads // 4
    lax.fori_loop(0, half, inside, 0)

    drain(r1, s1_recv)
    total = r1[0].astype(F32)
    for i in range(1, row):
        total = total + r1[i].astype(F32)
    tot[...] = total.astype(BF)
    pltpu.make_async_copy(tot, r2.at[y], s2_recv).start()

    def phase2(i, _):
        yy = lax.rem(y + i, ny)
        remote(tot, r2.at[y], s2_send, s2_recv, seq(yy, z, c)).start()
        return 0

    lax.fori_loop(1, ny, phase2, 0)

    pa, pb = 2 * c, 2 * c + 1
    sib = seq(y, z, 1 - c)

    def a_block(yy):
        return w_all.at[pa, yy]

    def b_block(zz):
        return w_all.at[pb, :, zz]

    def a_half(yy, h):
        return w_all.at[pa, yy, pl.ds(h * (nz // 2), nz // 2)]

    def b_half(zz, h):
        return w_all.at[pb, pl.ds(h * (ny // 2), ny // 2), zz]

    def mod_y(v):
        return lax.rem(v + 2 * ny, ny)

    def mod_z(v):
        return lax.rem(v + 2 * nz, nz)

    def to_sibling(block):
        remote(block, block, sib_send, sib_recv, sib).start()

    ring = []

    def ring_copy(axis, way, step):
        size, mod, at = (ny, mod_y, y) if axis == 0 else (nz, mod_z, z)
        block, part = (a_block, a_half) if axis == 0 else (b_block, b_half)
        sign = 1 if way == 0 else -1
        origin = mod(at - sign * (step - 1))
        target = mod(at + sign)
        dev = seq(target, z, c) if axis == 0 else seq(y, target, c)
        ref = part(origin, way) if 2 * step == size else block(origin)
        return remote(
            ref, ref, ring_send.at[axis, way, step - 1], ring_recv.at[axis, way, step - 1], dev
        )

    def ring_got(axis, way, step):
        size, mod, at = (ny, mod_y, y) if axis == 0 else (nz, mod_z, z)
        block, part = (a_block, a_half) if axis == 0 else (b_block, b_half)
        origin = mod(at - step if way == 0 else at + step)
        ref = part(origin, way) if 2 * step == size else block(origin)
        drain(ref, ring_recv.at[axis, way, step - 1])
        return ref

    def ring_step(axis, step):
        size = ny if axis == 0 else nz
        if step > size // 2:
            return
        for way in (0, 1):
            got = ring_got(axis, way, step)
            if 2 * (step + 1) <= size:
                ring_copy(axis, way, step + 1).start()
            to_sibling(got)

    drain(w_all.at[pa, y], w1_recv.at[0])
    for way in (0, 1):
        ring_copy(0, way, 1).start()
    drain(w_all.at[pb, :, z], w1_recv.at[1])
    for way in (0, 1):
        ring_copy(1, way, 1).start()
    to_sibling(a_block(y))
    to_sibling(b_block(z))

    lax.fori_loop(half, heads // 2, inside, 0)

    drain(r2, s2_recv)
    run = jnp.zeros(total.shape, F32)
    for yy in range(ny):
        run = run + jnp.where(yy < y, r2[yy].astype(F32), 0.0)
    for i in range(row):
        p_out[i] = run.astype(BF)
        if i < row - 1:
            run = run + r1[i].astype(F32)
    pltpu.make_async_copy(p_out.at[at_row], r3.at[at_row], s3_recv).start()

    def phase3(i, _):
        to = lax.rem(at_row + i, row)
        remote(p_out.at[to], r3.at[at_row], s3_send, s3_recv, y * row + to).start()
        return 0

    lax.fori_loop(1, row, phase3, 0)

    for axis in (0, 1):
        ring_step(axis, 1)

    eye = lax.broadcasted_iota(jnp.int32, (length, length), 0) == lax.broadcasted_iota(
        jnp.int32, (length, length), 1
    )
    below = lax.broadcasted_iota(jnp.int32, (length, length), 1) < lax.broadcasted_iota(
        jnp.int32, (length, length), 0
    )
    above = lax.broadcasted_iota(jnp.int32, (length, length), 0) < lax.broadcasted_iota(
        jnp.int32, (length, length), 1
    )

    def column(r):
        return jnp.sum(jnp.where(eye, r, 0.0), axis=1, keepdims=True)

    id_row = [ids_ref[j : j + 1, :].astype(F32) for j in range(TOP)]
    id_col = [column(r) for r in id_row]
    gate_col = [column(gates_ref[j : j + 1, :]) for j in range(TOP)]
    place_row, place_col = [], []
    for j in range(TOP):
        row_count, col_count = 0.0, 0.0
        for i in range(TOP):
            row_count = row_count + jnp.where(above & (id_col[i] == id_row[j]), 1.0, 0.0)
            col_count = col_count + jnp.where(below & (id_col[j] == id_row[i]), 1.0, 0.0)
        place_row.append(id_row[j] * CAP + jnp.sum(row_count, axis=0, keepdims=True))
        place_col.append(id_col[j] * CAP + jnp.sum(col_count, axis=1, keepdims=True))
    rows = n * CAP
    r_iota = lax.broadcasted_iota(jnp.int32, (rows, length), 0).astype(F32)
    spread = jnp.where(
        (r_iota == place_row[0]) | (r_iota == place_row[1]), 1.0, 0.0
    ).astype(BF)

    for axis in (0, 1):
        ring_step(axis, 2)

    drain(r3, s3_recv)
    position = me * length + lax.broadcasted_iota(jnp.int32, (length, 1), 0)
    scaling = lax.rsqrt((position.astype(F32) + 1.0) * dk)
    for p in range(heads // 2):
        earlier = dot(two_heads(p), r3[2 * p : 2 * p + 2].reshape(2 * dk, dv))
        for h in range(2):
            cols = slice((2 * p + h) * dv, (2 * p + h + 1) * dv)
            attended[:, cols] = (
                (intra[:, cols] + earlier[h * length : (h + 1) * length]) * scaling
            ).astype(BF)

    for step in range(3, max(ny, nz) // 2 + 1):
        for axis in (0, 1):
            ring_step(axis, step)
    drain(w_all.at[pl.ds(2 * (1 - c), 2)], sib_recv)

    projected = jnp.zeros((length, width), F32)
    for part in range(4):
        projected = projected + dot(
            attended[:, part * quarter : (part + 1) * quarter],
            w_all[part].reshape(width, quarter),
            ((1,), (1,)),
        )
    hidden = (res_ref[...].astype(F32) + projected).astype(BF)
    hidden_float = hidden.astype(F32)
    intra[:, :width] = hidden_float
    normed = (
        hidden_float
        * lax.rsqrt(jnp.mean(hidden_float * hidden_float, axis=-1, keepdims=True) + 1e-06)
    ).astype(BF)
    xb[...] = dot(spread, normed).astype(BF).reshape(n, CAP, width)

    def offset(i):
        j = lax.rem(i * 37, n)
        return j // row, lax.rem(j // 2, nz), lax.rem(j, 2)

    def ahead(i):
        dy, dz, dc = offset(i)
        return seq(lax.rem(y + dy, ny), lax.rem(z + dz, nz), lax.rem(c + dc, 2))

    def behind(i):
        dy, dz, dc = offset(i)
        return seq(lax.rem(y - dy + ny, ny), lax.rem(z - dz + nz, nz), lax.rem(c - dc + 2, 2))

    per = n // GROUPS
    pltpu.make_async_copy(xb.at[me], xr.at[0], x_recv.at[0]).start()

    def dispatch(i, _):
        to = ahead(i)
        remote(xb.at[to], xr.at[i], x_send, x_recv.at[i // per], to).start()
        return 0

    lax.fori_loop(1, n, dispatch, 0)

    load_in.wait()
    load_out.wait()

    def expert(g):
        lo = g * per
        drain(xr.at[pl.ds(lo, per)], x_recv.at[g])
        x = xr[pl.ds(lo, per)].reshape(per * CAP, width)
        act = dot(x, win[...])
        gate, up = act[:, :he], act[:, he:]
        inner = (gate / (1.0 + jnp.exp(-gate)) * up).astype(BF)
        yb[pl.ds(lo, per)] = dot(inner, wout[...]).astype(BF).reshape(per, CAP, width)

    def give_back(i, _):
        to = behind(i)
        remote(yb.at[i], ret.at[me], y_send, y_recv, to).start()
        return 0

    expert(0)
    pltpu.make_async_copy(yb.at[0], ret.at[me], y_recv).start()
    lax.fori_loop(1, per, give_back, 0)

    def group(g, _):
        expert(g)
        lax.fori_loop(g * per, (g + 1) * per, give_back, 0)
        return 0

    lax.fori_loop(1, GROUPS, group, 0)

    r_lane = lax.broadcasted_iota(jnp.int32, (length, rows), 1).astype(F32)
    picks = [jnp.where(r_lane == place_col[j], 1.0, 0.0).astype(BF) for j in range(TOP)]
    drain(ret, y_recv)
    back = ret[...].reshape(rows, width)
    combined = dot(picks[0], back) * gate_col[0] + dot(picks[1], back) * gate_col[1]
    o_ref[...] = (intra[:, :width] + combined).astype(BF)

    drain(s_loc.at[pl.ds(0, row - 1)], s1_send)
    drain(r2.at[pl.ds(0, ny - 1)], s2_send)
    drain(p_out.at[pl.ds(0, row - 1)], s3_send)
    for _ in range(2):
        drain(w_loc.at[0], w1_send)
    for _ in range(row - 2 + 2 * ny - 2):
        drain(w_loc.at[0], w1_send)
    for axis, size in ((0, ny), (1, nz)):
        for step in range(1, size // 2 + 1):
            for way in (0, 1):
                ring_copy(axis, way, step).wait_send()
    drain(w_all.at[pl.ds(2 * c, 2)], sib_send)
    drain(xb.at[pl.ds(0, n - 1)], x_send)
    drain(yb.at[pl.ds(0, n - 1)], y_send)


def layer(ny, nz, heads, dk, dv, q, k, v, res, wt, w_in, w_out, ids, gates):
    n = ny * nz * 2
    row = nz * 2
    length, width = res.shape
    cols = wt.shape[0]
    quarter = heads * dv // 4
    vmem = pl.BlockSpec(memory_space=pltpu.VMEM)
    hbm = pl.BlockSpec(memory_space=pl.ANY)
    steps = max(ny, nz) // 2
    dma = pltpu.SemaphoreType.DMA
    rows = (n, CAP, width)
    return pl.pallas_call(
        functools.partial(layer_kernel, ny, nz, heads, dk, dv),
        out_shape=jax.ShapeDtypeStruct((length, width), BF),
        in_specs=[vmem] * 5 + [hbm] * 2 + [vmem] * 2,
        out_specs=vmem,
        scratch_shapes=[
            pltpu.VMEM((heads, dk, dv), BF),
            pltpu.VMEM((dk, dv), BF),
            pltpu.VMEM((row, dk, dv), BF),
            pltpu.VMEM((row, dk, dv), BF),
            pltpu.VMEM((ny, dk, dv), BF),
            pltpu.VMEM((row, dk, dv), BF),
            pltpu.VMEM((4, cols, quarter), BF),
            pltpu.VMEM((4, ny, nz, 2, cols, quarter), BF),
            pltpu.VMEM((length, heads * dv), F32),
            pltpu.VMEM((length, heads * dv), BF),
            pltpu.VMEM(w_in.shape, BF),
            pltpu.VMEM(w_out.shape, BF),
            pltpu.VMEM(rows, BF),
            pltpu.VMEM(rows, BF),
            pltpu.VMEM(rows, BF),
            pltpu.VMEM(rows, BF),
            dma,
            dma,
            dma,
            dma,
            dma,
            dma,
            dma,
            dma((2,)),
            dma((2, 2, steps)),
            dma((2, 2, steps)),
            dma,
            dma,
            dma,
            dma((GROUPS,)),
            dma,
            dma,
            dma((2,)),
        ],
        compiler_params=pltpu.CompilerParams(
            collective_id=0, has_side_effects=True, vmem_limit_bytes=40 * 2**20
        ),
        name="layer",
    )(q, k, v, res, wt, w_in, w_out, ids, gates)


def solution(mesh, ny=8, nz=8, heads=16, dk=64, dv=128):
    def per_device(q, k, v, res, w, w_in, w_out, ids, gates):
        return layer(
            ny, nz, heads, dk, dv, q, k, v, res, w.T, w_in[0], w_out[0], ids.T, gates.T
        )

    tokens = P(("win", "seq"), None)
    experts = P("seq", None, None)
    return jax.shard_map(
        per_device,
        mesh=mesh,
        in_specs=(tokens,) * 4 + (P(None, "seq"), experts, experts, tokens, tokens),
        out_specs=tokens,
        check_vma=False,
    )
```

```python
import functools

import jax
import jax.numpy as jnp
from jax import lax
from jax.experimental import pallas as pl
from jax.experimental.pallas import tpu as pltpu
from jax.sharding import PartitionSpec as P

TOP = 2
CAP = 4
GROUPS = 4
MESH = pl.DeviceIdType.MESH
BF = jnp.bfloat16
F32 = jnp.float32


def dot(a, b, dims=((1,), (0,))):
    return lax.dot_general(a, b, (dims, ((), ())), preferred_element_type=F32)


def layer_kernel(
    ny,
    nz,
    heads,
    dk,
    dv,
    q_hbm,
    k_hbm,
    v_hbm,
    res_hbm,
    wt_hbm,
    win_hbm,
    wout_hbm,
    ids_hbm,
    gates_hbm,
    o_ref,
    q_ref,
    k_ref,
    v_ref,
    res_ref,
    wt_ref,
    ids_ref,
    gates_ref,
    s_loc,
    s_sib,
    s_pair,
    s_pair_out,
    tot,
    p_out,
    r1,
    r2,
    r3,
    prefix,
    w_loc,
    w_all,
    intra,
    attended,
    win,
    wout,
    xb,
    xr,
    yb,
    ret,
    s0_send,
    s0_recv,
    s1_send,
    s1_recv,
    s2_send,
    s2_recv,
    s3_send,
    s3_recv,
    s4_send,
    s4_recv,
    w0_send,
    w0_recv,
    w1_send,
    w1_recv,
    met,
    ring_send,
    ring_recv,
    sib_send,
    sib_recv,
    x_send,
    x_recv,
    y_send,
    y_recv,
    win_sem,
):
    n = ny * nz * 2
    row = nz * 2
    length = q_ref.shape[0]
    width = res_ref.shape[1]
    he = wout.shape[0]
    quarter = w_loc.shape[2]
    me = lax.axis_index("seq")
    y, z, c = me // row, lax.rem(me // 2, nz), lax.rem(me, 2)

    def seq(yy, zz, cc):
        return yy * row + zz * 2 + cc

    def remote(src, dst, ssem, rsem, dev):
        return pltpu.make_async_remote_copy(
            src_ref=src,
            dst_ref=dst,
            send_sem=ssem,
            recv_sem=rsem,
            device_id={"seq": dev},
            device_id_type=MESH,
        )

    def drain(ref, sem):
        pltpu.make_async_copy(ref, ref, sem).wait()

    loads = [
        pltpu.make_async_copy(src, dst, win_sem.at[i])
        for i, (src, dst) in enumerate(
            (
                (k_hbm, k_ref),
                (v_hbm, v_ref),
                (wt_hbm, wt_ref),
                (q_hbm, q_ref),
                (ids_hbm, ids_ref),
                (gates_hbm, gates_ref),
                (res_hbm, res_ref),
                (win_hbm, win),
                (wout_hbm, wout),
            )
        )
    ]
    for load in loads:
        load.start()
    barrier = pltpu.get_barrier_semaphore()

    def greet(dev):
        pl.semaphore_signal(barrier, inc=1, device_id={"seq": dev}, device_id_type=MESH)

    def greet_row(i, _):
        greet(seq(y, lax.rem(z + i, nz), c))
        return 0

    def greet_column(i, _):
        greet(seq(lax.rem(y + i, ny), z, c))
        return 0

    sib = seq(y, z, 1 - c)
    greet(sib)
    lax.fori_loop(1, nz, greet_row, 0)
    lax.fori_loop(1, ny, greet_column, 0)

    loads[0].wait()
    loads[1].wait()

    def states(p, _):
        kp = k_ref[:, pl.ds(pl.multiple_of(p * 2 * dk, 2 * dk), 2 * dk)]
        vp = v_ref[:, pl.ds(pl.multiple_of(p * 2 * dv, 2 * dv), 2 * dv)]
        kv = dot(kp, vp, ((0,), (0,)))
        s_loc[2 * p] = kv[:dk, :dv].astype(BF)
        s_loc[2 * p + 1] = kv[dk:, dv:].astype(BF)
        return 0

    lax.fori_loop(0, heads // 2, states, 0)
    loads[2].wait()
    for part in range(4):
        w_loc[part] = wt_ref[:, part * quarter : (part + 1) * quarter]

    pl.semaphore_wait(barrier, nz + ny - 1)

    hh = heads // 2
    own, other = c * hh, (1 - c) * hh
    pa, pb = 2 * c, 2 * c + 1
    first_core = c == 0
    remote(s_loc.at[pl.ds(other, hh)], s_sib, s0_send, s0_recv, sib).start()

    def w_join(part, which):
        pltpu.make_async_copy(
            w_loc.at[part], w_all.at[part, y, z, c], w0_recv.at[which]
        ).start()

    for which in range(2):
        part = 2 * (1 - c) + which
        remote(
            w_loc.at[part], w_all.at[part, y, z, c], w0_send, w0_recv.at[which], sib
        ).start()
    w_join(pa, 0)
    w_join(pb, 1)

    def tell(cc, yy):
        pl.semaphore_signal(
            met, inc=1, device_id={"seq": seq(yy, z, cc)}, device_id_type=MESH
        )

    def tell_column(i, _):
        tell(c, lax.rem(y + i, ny))
        return 0

    lax.fori_loop(1, ny, tell_column, 0)

    drain(s_sib, s0_recv)
    for i in range(hh):
        both = s_loc[own + i].astype(F32) + s_sib[i].astype(F32)
        s_pair[i] = both.astype(BF)
    pltpu.make_async_copy(s_pair.at[z], r1.at[z], s1_recv).start()

    def phase1(i, _):
        to = lax.rem(z + i, nz)
        remote(s_pair.at[to], r1.at[z], s1_send, s1_recv, seq(y, to, c)).start()
        return 0

    lax.fori_loop(1, nz, phase1, 0)

    def along_z(i, _):
        ref = w_all.at[pa, y, z]
        remote(ref, ref, w1_send.at[0], w1_recv.at[0], seq(y, lax.rem(z + i, nz), c)).start()
        return 0

    def along_y(i, _):
        ref = w_all.at[pb, y, z]
        remote(ref, ref, w1_send.at[1], w1_recv.at[1], seq(lax.rem(y + i, ny), z, c)).start()
        return 0

    drain(w_all.at[pa, y, z], w0_recv.at[0])
    lax.fori_loop(1, nz, along_z, 0)
    drain(w_all.at[pb, y, z], w0_recv.at[1])
    lax.fori_loop(1, ny, along_y, 0)

    t_row = lax.broadcasted_iota(jnp.int32, (2 * length, length), 0)
    t_col = lax.broadcasted_iota(jnp.int32, (2 * length, length), 1)
    causal = lax.rem(t_row, length) >= t_col
    first = lax.broadcasted_iota(jnp.int32, (length, 2 * dk), 1) < dk

    def two_heads(p):
        qp = q_ref[:, pl.ds(pl.multiple_of(p * 2 * dk, 2 * dk), 2 * dk)]
        zero = jnp.zeros_like(qp)
        return jnp.concatenate(
            [jnp.where(first, qp, zero), jnp.where(first, zero, qp)], axis=0
        )

    def inside(p, _):
        kp = k_ref[:, pl.ds(pl.multiple_of(p * 2 * dk, 2 * dk), 2 * dk)]
        at = pl.multiple_of(p * 2 * dv, 2 * dv)
        scores = dot(two_heads(p), kp, ((1,), (1,)))
        scores = jnp.where(causal, scores, 0.0).astype(BF)
        vp = v_ref[:, pl.ds(at, 2 * dv)]
        intra[:, pl.ds(at, dv)] = dot(scores[:length], vp[:, :dv])
        intra[:, pl.ds(pl.multiple_of(at + dv, dv), dv)] = dot(scores[length:], vp[:, dv:])
        return 0

    loads[3].wait()
    half = heads // 4
    lax.fori_loop(0, half, inside, 0)

    drain(r1, s1_recv)
    total = r1[0].astype(F32)
    for i in range(1, nz):
        total = total + r1[i].astype(F32)
    tot[...] = total.astype(BF)
    pltpu.make_async_copy(tot, r2.at[y], s2_recv).start()

    def phase2(i, _):
        yy = lax.rem(y + i, ny)
        remote(tot, r2.at[y], s2_send, s2_recv, seq(yy, z, c)).start()
        return 0

    lax.fori_loop(1, ny, phase2, 0)

    def mod_y(v):
        return lax.rem(v + 2 * ny, ny)

    def mod_z(v):
        return lax.rem(v + 2 * nz, nz)

    def piece(axis, origin, h):
        if axis == 0:
            return w_all.at[pa, origin, pl.ds(h * (nz // 2), nz // 2)]
        return w_all.at[pb, pl.ds(h * (ny // 2), ny // 2), origin]

    def pieces(axis, way, step):
        size = ny if axis == 0 else nz
        if 2 * step > size:
            return ()
        return (way,) if 2 * step == size else (way, 1 - way)

    def to_sibling(ref):
        remote(ref, ref, sib_send, sib_recv, sib).start()

    def ring_copy(axis, way, step, h):
        mod, at = (mod_y, y) if axis == 0 else (mod_z, z)
        sign = 1 if way == 0 else -1
        ref = piece(axis, mod(at - sign * (step - 1)), h)
        dev = seq(mod(at + sign), z, c) if axis == 0 else seq(y, mod(at + sign), c)
        place = (axis, way, step - 1, h)
        return remote(ref, ref, ring_send.at[place], ring_recv.at[place], dev)

    def ring_step(axis, step):
        mod, at = (mod_y, y) if axis == 0 else (mod_z, z)
        for turn in range(2):
            for way in (0, 1):
                if turn < len(pieces(axis, way, step)):
                    h = pieces(axis, way, step)[turn]
                    ref = piece(axis, mod(at - step if way == 0 else at + step), h)
                    drain(ref, ring_recv.at[axis, way, step - 1, h])
                    if h in pieces(axis, way, step + 1):
                        ring_copy(axis, way, step + 1, h).start()
                    to_sibling(ref)

    def ring_open(axis):
        for turn in range(2):
            for way in (0, 1):
                if turn < len(pieces(axis, way, 1)):
                    ring_copy(axis, way, 1, pieces(axis, way, 1)[turn]).start()

    drain(w_all.at[pa, y, pl.ds(0, nz - 1)], w1_recv.at[0])
    ring_open(0)
    drain(w_all.at[pb, pl.ds(0, ny - 1), z], w1_recv.at[1])
    ring_open(1)
    to_sibling(w_all.at[pa, y])
    to_sibling(w_all.at[pb, :, z])

    drain(r2, s2_recv)
    run = jnp.zeros(total.shape, F32)
    for yy in range(ny):
        run = run + jnp.where(yy < y, r2[yy].astype(F32), 0.0)
    for i in range(nz):
        p_out[i] = run.astype(BF)
        if i < nz - 1:
            run = run + r1[i].astype(F32)
    pltpu.make_async_copy(p_out.at[z], r3.at[z], s3_recv).start()

    def phase3(i, _):
        to = lax.rem(z + i, nz)
        remote(p_out.at[to], r3.at[z], s3_send, s3_recv, seq(y, to, c)).start()
        return 0

    lax.fori_loop(1, nz, phase3, 0)

    for axis in (0, 1):
        ring_step(axis, 1)
    lax.fori_loop(half, heads // 2, inside, 0)

    drain(r3, s3_recv)
    for i in range(hh):
        chip = r3[i].astype(F32)
        theirs = chip + jnp.where(first_core, s_loc[own + i].astype(F32), 0.0)
        s_pair_out[i] = theirs.astype(BF)
    remote(s_pair_out, prefix.at[pl.ds(own, hh)], s4_send, s4_recv, sib).start()
    for i in range(hh):
        chip = r3[i].astype(F32)
        mine = chip + jnp.where(first_core, 0.0, s_sib[i].astype(F32))
        prefix[own + i] = mine.astype(BF)

    for axis in (0, 1):
        ring_step(axis, 2)

    eye = lax.broadcasted_iota(jnp.int32, (length, length), 0) == lax.broadcasted_iota(
        jnp.int32, (length, length), 1
    )
    below = lax.broadcasted_iota(jnp.int32, (length, length), 1) < lax.broadcasted_iota(
        jnp.int32, (length, length), 0
    )
    above = lax.broadcasted_iota(jnp.int32, (length, length), 0) < lax.broadcasted_iota(
        jnp.int32, (length, length), 1
    )

    for load in loads[4:7]:
        load.wait()

    def column(r):
        return jnp.sum(jnp.where(eye, r, 0.0), axis=1, keepdims=True)

    id_row = [ids_ref[j : j + 1, :].astype(F32) for j in range(TOP)]
    id_col = [column(r) for r in id_row]
    gate_col = [column(gates_ref[j : j + 1, :]) for j in range(TOP)]
    place_row, place_col = [], []
    for j in range(TOP):
        row_count, col_count = 0.0, 0.0
        for i in range(TOP):
            row_count = row_count + jnp.where(above & (id_col[i] == id_row[j]), 1.0, 0.0)
            col_count = col_count + jnp.where(below & (id_col[j] == id_row[i]), 1.0, 0.0)
        place_row.append(id_row[j] * CAP + jnp.sum(row_count, axis=0, keepdims=True))
        place_col.append(id_col[j] * CAP + jnp.sum(col_count, axis=1, keepdims=True))
    rows = n * CAP
    r_iota = lax.broadcasted_iota(jnp.int32, (rows, length), 0).astype(F32)
    spread = jnp.where(
        (r_iota == place_row[0]) | (r_iota == place_row[1]), 1.0, 0.0
    ).astype(BF)

    position = me * length + lax.broadcasted_iota(jnp.int32, (length, 1), 0)
    scaling = lax.rsqrt((position.astype(F32) + 1.0) * dk)

    def before(p):
        past = prefix[pl.ds(2 * p, 2)].reshape(2 * dk, dv)
        earlier = dot(two_heads(p), past)
        for h in range(2):
            cols = pl.ds(pl.multiple_of((2 * p + h) * dv, dv), dv)
            attended[:, cols] = (
                (intra[:, cols] + earlier[h * length : (h + 1) * length]) * scaling
            ).astype(BF)

    for p in range(hh // 2):
        before(own // 2 + p)
    drain(prefix.at[pl.ds(other, hh)], s4_recv)
    for p in range(hh // 2):
        before(other // 2 + p)

    for step in range(3, max(ny, nz) // 2 + 1):
        for axis in (0, 1):
            ring_step(axis, step)

    def project(part):
        cols = pl.ds(pl.multiple_of(part * quarter, quarter), quarter)
        return dot(attended[:, cols], w_all[part].reshape(width, quarter), ((1,), (1,)))

    projected = project(pa) + project(pb)
    drain(w_all.at[pl.ds(2 * (1 - c), 2)], sib_recv)
    projected = projected + (project(2 * (1 - c)) + project(2 * (1 - c) + 1))
    hidden = (res_ref[...].astype(F32) + projected).astype(BF)
    hidden_float = hidden.astype(F32)
    intra[:, :width] = hidden_float
    normed = (
        hidden_float
        * lax.rsqrt(jnp.mean(hidden_float * hidden_float, axis=-1, keepdims=True) + 1e-06)
    ).astype(BF)
    xb[...] = dot(spread, normed).astype(BF).reshape(n, CAP, width)

    def offset(i):
        j = lax.rem(i * 37, n)
        return j // row, lax.rem(j // 2, nz), lax.rem(j, 2)

    def ahead(i):
        dy, dz, dc = offset(i)
        return seq(lax.rem(y + dy, ny), lax.rem(z + dz, nz), lax.rem(c + dc, 2))

    def behind(i):
        dy, dz, dc = offset(i)
        return seq(lax.rem(y - dy + ny, ny), lax.rem(z - dz + nz, nz), lax.rem(c - dc + 2, 2))

    per = n // GROUPS
    pl.semaphore_wait(met, ny - 1)
    pltpu.make_async_copy(xb.at[me], xr.at[0], x_recv.at[0]).start()

    def dispatch(i, _):
        to = ahead(i)
        remote(xb.at[to], xr.at[i], x_send, x_recv.at[i // per], to).start()
        return 0

    lax.fori_loop(1, n, dispatch, 0)

    loads[7].wait()
    loads[8].wait()

    def expert(g):
        lo = g * per
        drain(xr.at[pl.ds(lo, per)], x_recv.at[g])
        x = xr[pl.ds(lo, per)].reshape(per * CAP, width)
        act = dot(x, win[...])
        gate, up = act[:, :he], act[:, he:]
        inner = (gate / (1.0 + jnp.exp(-gate)) * up).astype(BF)
        yb[pl.ds(lo, per)] = dot(inner, wout[...]).astype(BF).reshape(per, CAP, width)

    def give_back(i, _):
        to = behind(i)
        remote(yb.at[i], ret.at[me], y_send, y_recv, to).start()
        return 0

    expert(0)
    pltpu.make_async_copy(yb.at[0], ret.at[me], y_recv).start()
    lax.fori_loop(1, per, give_back, 0)

    def group(g, _):
        expert(g)
        lax.fori_loop(g * per, (g + 1) * per, give_back, 0)
        return 0

    lax.fori_loop(1, GROUPS, group, 0)

    r_lane = lax.broadcasted_iota(jnp.int32, (length, rows), 1).astype(F32)
    picks = [jnp.where(r_lane == place_col[j], 1.0, 0.0).astype(BF) for j in range(TOP)]
    drain(ret, y_recv)
    back = ret[...].reshape(rows, width)
    combined = dot(picks[0], back) * gate_col[0] + dot(picks[1], back) * gate_col[1]
    o_ref[...] = (intra[:, :width] + combined).astype(BF)

    drain(s_sib, s0_send)
    drain(r1.at[pl.ds(0, nz - 1)], s1_send)
    drain(r2.at[pl.ds(0, ny - 1)], s2_send)
    drain(r3.at[pl.ds(0, nz - 1)], s3_send)
    drain(s_sib, s4_send)
    drain(w_loc.at[pl.ds(0, 2)], w0_send)
    drain(w_all.at[pa, y, pl.ds(0, nz - 1)], w1_send.at[0])
    drain(w_all.at[pb, pl.ds(0, ny - 1), z], w1_send.at[1])
    for axis in (0, 1):
        for step in range(1, max(ny, nz) // 2 + 1):
            for way in (0, 1):
                for h in pieces(axis, way, step):
                    ring_copy(axis, way, step, h).wait_send()
    drain(w_all.at[pl.ds(2 * c, 2)], sib_send)
    drain(xb.at[pl.ds(0, n - 1)], x_send)
    drain(yb.at[pl.ds(0, n - 1)], y_send)


def layer(ny, nz, heads, dk, dv, q, k, v, res, wt, w_in, w_out, ids, gates):
    n = ny * nz * 2
    length, width = res.shape
    cols = wt.shape[0]
    quarter = heads * dv // 4
    vmem = pl.BlockSpec(memory_space=pltpu.VMEM)
    hbm = pl.BlockSpec(memory_space=pl.ANY)
    steps = max(ny, nz) // 2
    dma = pltpu.SemaphoreType.DMA
    rows = (n, CAP, width)
    return pl.pallas_call(
        functools.partial(layer_kernel, ny, nz, heads, dk, dv),
        out_shape=jax.ShapeDtypeStruct((length, width), BF),
        in_specs=[hbm] * 9,
        out_specs=vmem,
        scratch_shapes=[
            *[pltpu.VMEM(a.shape, a.dtype) for a in (q, k, v, res, wt, ids, gates)],
            pltpu.VMEM((heads, dk, dv), BF),
            pltpu.VMEM((nz, dk, dv), BF),
            pltpu.VMEM((nz, dk, dv), BF),
            pltpu.VMEM((nz, dk, dv), BF),
            pltpu.VMEM((dk, dv), BF),
            pltpu.VMEM((nz, dk, dv), BF),
            pltpu.VMEM((nz, dk, dv), BF),
            pltpu.VMEM((ny, dk, dv), BF),
            pltpu.VMEM((nz, dk, dv), BF),
            pltpu.VMEM((heads, dk, dv), BF),
            pltpu.VMEM((4, cols, quarter), BF),
            pltpu.VMEM((4, ny, nz, 2, cols, quarter), BF),
            pltpu.VMEM((length, heads * dv), F32),
            pltpu.VMEM((length, heads * dv), BF),
            pltpu.VMEM(w_in.shape, BF),
            pltpu.VMEM(w_out.shape, BF),
            pltpu.VMEM(rows, BF),
            pltpu.VMEM(rows, BF),
            pltpu.VMEM(rows, BF),
            pltpu.VMEM(rows, BF),
            *[dma] * 11,
            dma((2,)),
            dma((2,)),
            dma((2,)),
            pltpu.SemaphoreType.REGULAR,
            dma((2, 2, steps, 2)),
            dma((2, 2, steps, 2)),
            dma,
            dma,
            dma,
            dma((GROUPS,)),
            dma,
            dma,
            dma((9,)),
        ],
        compiler_params=pltpu.CompilerParams(
            collective_id=0, has_side_effects=True, vmem_limit_bytes=60 * 2**20
        ),
        name="layer",
    )(q, k, v, res, wt, w_in, w_out, ids, gates)


def solution(mesh, ny=8, nz=8, heads=16, dk=64, dv=128):
    def per_device(q, k, v, res, w, w_in, w_out, ids, gates):
        return layer(
            ny, nz, heads, dk, dv, q, k, v, res, w.T, w_in[0], w_out[0], ids.T, gates.T
        )

    tokens = P(("win", "seq"), None)
    experts = P("seq", None, None)
    return jax.shard_map(
        per_device,
        mesh=mesh,
        in_specs=(tokens,) * 4 + (P(None, "seq"), experts, experts, tokens, tokens),
        out_specs=tokens,
        check_vma=False,
    )
```

```python
import functools

import jax
import jax.numpy as jnp
from jax import lax
from jax.experimental import pallas as pl
from jax.experimental.pallas import tpu as pltpu
from jax.sharding import PartitionSpec as P

TOP = 2
CAP = 4
GROUPS = 4
MESH = pl.DeviceIdType.MESH
BF = jnp.bfloat16
F32 = jnp.float32


def dot(a, b, dims=((1,), (0,))):
    return lax.dot_general(a, b, (dims, ((), ())), preferred_element_type=F32)


def layer_kernel(
    ny,
    nz,
    heads,
    dk,
    dv,
    q_hbm,
    k_hbm,
    v_hbm,
    res_hbm,
    wt_hbm,
    win_hbm,
    wout_hbm,
    ids_hbm,
    gates_hbm,
    o_ref,
    q_ref,
    k_ref,
    v_ref,
    res_ref,
    wt_ref,
    ids_ref,
    gates_ref,
    s_loc,
    s_sib,
    s_pair,
    s_pair_out,
    tot,
    p_out,
    r1,
    r2,
    r3,
    prefix,
    w_loc,
    w_all,
    intra,
    attended,
    win,
    wout,
    xb,
    xr,
    yb,
    ret,
    s0_send,
    s0_recv,
    s1_send,
    s1_recv,
    s2_send,
    s2_recv,
    s3_send,
    s3_recv,
    s4_send,
    s4_recv,
    w1_send,
    w1_recv,
    met,
    ring_send,
    ring_recv,
    sib_send,
    sib_recv,
    x_send,
    x_recv,
    y_send,
    y_recv,
    win_sem,
):
    n = ny * nz * 2
    row = nz * 2
    length = q_ref.shape[0]
    width = res_ref.shape[1]
    he = wout.shape[0]
    quarter = w_loc.shape[2]
    cut = min(4, ny, nz)
    me = lax.axis_index("seq")
    y, z, c = me // row, lax.rem(me // 2, nz), lax.rem(me, 2)
    at_row = lax.rem(me, row)

    def seq(yy, zz, cc):
        return yy * row + zz * 2 + cc

    def remote(src, dst, ssem, rsem, dev):
        return pltpu.make_async_remote_copy(
            src_ref=src,
            dst_ref=dst,
            send_sem=ssem,
            recv_sem=rsem,
            device_id={"seq": dev},
            device_id_type=MESH,
        )

    def drain(ref, sem):
        pltpu.make_async_copy(ref, ref, sem).wait()

    loads = [
        pltpu.make_async_copy(src, dst, win_sem.at[i])
        for i, (src, dst) in enumerate(
            (
                (k_hbm, k_ref),
                (v_hbm, v_ref),
                (wt_hbm, wt_ref),
                (q_hbm, q_ref),
                (ids_hbm, ids_ref),
                (gates_hbm, gates_ref),
                (res_hbm, res_ref),
                (win_hbm, win),
                (wout_hbm, wout),
            )
        )
    ]
    for load in loads:
        load.start()
    barrier = pltpu.get_barrier_semaphore()

    def greet(dev):
        pl.semaphore_signal(barrier, inc=1, device_id={"seq": dev}, device_id_type=MESH)

    def greet_row(i, _):
        greet(y * row + lax.rem(at_row + i, row))
        return 0

    def greet_column(i, _):
        greet(seq(lax.rem(y + i // 2, ny), z, lax.rem(c + i, 2)))
        return 0

    sib = seq(y, z, 1 - c)
    lax.fori_loop(1, row, greet_row, 0)
    lax.fori_loop(2, 2 * ny, greet_column, 0)

    loads[2].wait()
    for part in range(4):
        w_loc[part] = wt_ref[:, part * quarter : (part + 1) * quarter]
    pl.semaphore_wait(barrier, row + 2 * ny - 3)

    pa, pb = 2 * c, 2 * c + 1

    def keep(part, sem):
        pltpu.make_async_copy(w_loc.at[part], w_all.at[part, y, z, c], sem).start()

    def along_z(i, _):
        to = lax.rem(at_row + i, row)
        part = 2 * lax.rem(to, 2)
        remote(
            w_loc.at[part], w_all.at[part, y, z, c], w1_send.at[0], w1_recv.at[0], y * row + to
        ).start()
        return 0

    def along_y(i, _):
        cc = lax.rem(c + i, 2)
        part = 2 * cc + 1
        remote(
            w_loc.at[part],
            w_all.at[part, y, z, c],
            w1_send.at[1],
            w1_recv.at[1],
            seq(lax.rem(y + i // 2, ny), z, cc),
        ).start()
        return 0

    keep(pa, w1_recv.at[0])
    keep(pb, w1_recv.at[1])
    lax.fori_loop(1, row, along_z, 0)
    lax.fori_loop(1, 2 * ny, along_y, 0)

    loads[0].wait()
    loads[1].wait()

    for p in range(heads // 2):
        kp = k_ref[:, 2 * p * dk : 2 * (p + 1) * dk]
        kv = dot(kp, v_ref[:, 2 * p * dv : 2 * (p + 1) * dv], ((0,), (0,)))
        s_loc[2 * p] = kv[:dk, :dv].astype(BF)
        s_loc[2 * p + 1] = kv[dk:, dv:].astype(BF)

    hh = heads // 2
    own, other = c * hh, (1 - c) * hh
    first_core = c == 0
    remote(s_loc.at[pl.ds(other, hh)], s_sib, s0_send, s0_recv, sib).start()

    def tell(cc, yy):
        pl.semaphore_signal(
            met, inc=1, device_id={"seq": seq(yy, z, cc)}, device_id_type=MESH
        )

    def tell_column(i, _):
        tell(c, lax.rem(y + i, ny))
        return 0

    lax.fori_loop(1, ny, tell_column, 0)

    eye = lax.broadcasted_iota(jnp.int32, (length, length), 0) == lax.broadcasted_iota(
        jnp.int32, (length, length), 1
    )
    below = lax.broadcasted_iota(jnp.int32, (length, length), 1) < lax.broadcasted_iota(
        jnp.int32, (length, length), 0
    )
    above = lax.broadcasted_iota(jnp.int32, (length, length), 0) < lax.broadcasted_iota(
        jnp.int32, (length, length), 1
    )

    for load in loads[4:7]:
        load.wait()

    def column(r):
        return jnp.sum(jnp.where(eye, r, 0.0), axis=1, keepdims=True)

    id_row = [ids_ref[j : j + 1, :].astype(F32) for j in range(TOP)]
    id_col = [column(r) for r in id_row]
    gate_col = [column(gates_ref[j : j + 1, :]) for j in range(TOP)]
    place_row, place_col = [], []
    for j in range(TOP):
        row_count, col_count = 0.0, 0.0
        for i in range(TOP):
            row_count = row_count + jnp.where(above & (id_col[i] == id_row[j]), 1.0, 0.0)
            col_count = col_count + jnp.where(below & (id_col[j] == id_row[i]), 1.0, 0.0)
        place_row.append(id_row[j] * CAP + jnp.sum(row_count, axis=0, keepdims=True))
        place_col.append(id_col[j] * CAP + jnp.sum(col_count, axis=1, keepdims=True))
    rows = n * CAP
    r_iota = lax.broadcasted_iota(jnp.int32, (rows, length), 0).astype(F32)
    spread = jnp.where(
        (r_iota == place_row[0]) | (r_iota == place_row[1]), 1.0, 0.0
    ).astype(BF)

    drain(s_sib, s0_recv)
    for i in range(hh):
        both = s_loc[own + i].astype(F32) + s_sib[i].astype(F32)
        s_pair[i] = both.astype(BF)
    pltpu.make_async_copy(s_pair.at[z], r1.at[z], s1_recv).start()

    def phase1(i, _):
        to = lax.rem(z + i, nz)
        remote(s_pair.at[to], r1.at[z], s1_send, s1_recv, seq(y, to, c)).start()
        return 0

    lax.fori_loop(1, nz, phase1, 0)

    t_row = lax.broadcasted_iota(jnp.int32, (2 * length, length), 0)
    t_col = lax.broadcasted_iota(jnp.int32, (2 * length, length), 1)
    causal = lax.rem(t_row, length) >= t_col
    first = lax.broadcasted_iota(jnp.int32, (length, 2 * dk), 1) < dk

    def two_heads(p):
        qp = q_ref[:, pl.ds(pl.multiple_of(p * 2 * dk, 2 * dk), 2 * dk)]
        zero = jnp.zeros_like(qp)
        return jnp.concatenate(
            [jnp.where(first, qp, zero), jnp.where(first, zero, qp)], axis=0
        )

    def inside(p, _):
        kp = k_ref[:, pl.ds(pl.multiple_of(p * 2 * dk, 2 * dk), 2 * dk)]
        at = pl.multiple_of(p * 2 * dv, 2 * dv)
        scores = dot(two_heads(p), kp, ((1,), (1,)))
        scores = jnp.where(causal, scores, 0.0).astype(BF)
        vp = v_ref[:, pl.ds(at, 2 * dv)]
        intra[:, pl.ds(at, dv)] = dot(scores[:length], vp[:, :dv])
        intra[:, pl.ds(pl.multiple_of(at + dv, dv), dv)] = dot(scores[length:], vp[:, dv:])
        return 0

    loads[3].wait()
    half = heads // 4
    lax.fori_loop(0, half, inside, 0)

    def mod_y(v):
        return lax.rem(v + 2 * ny, ny)

    def mod_z(v):
        return lax.rem(v + 2 * nz, nz)

    def piece(axis, origin, h, many=1):
        if axis == 0:
            return w_all.at[pa, origin, pl.ds(h * (nz // cut), many * (nz // cut))]
        return w_all.at[pb, pl.ds(h * (ny // cut), many * (ny // cut)), origin]

    def pieces(axis, way, step):
        size = ny if axis == 0 else nz
        mine = tuple(range(way * cut // 2, (way + 1) * cut // 2))
        if 2 * step > size:
            return ()
        return mine if 2 * step == size else mine + tuple(set(range(cut)) - set(mine))

    def to_sibling(ref):
        remote(ref, ref, sib_send, sib_recv, sib).start()

    def ring_copy(axis, way, step, h):
        mod, at = (mod_y, y) if axis == 0 else (mod_z, z)
        sign = 1 if way == 0 else -1
        ref = piece(axis, mod(at - sign * (step - 1)), h)
        dev = seq(mod(at + sign), z, c) if axis == 0 else seq(y, mod(at + sign), c)
        place = (axis, way, step - 1, h)
        return remote(ref, ref, ring_send.at[place], ring_recv.at[place], dev)

    def ring_step(step):
        for turn in range(cut):
            for axis in (0, 1):
                mod, at = (mod_y, y) if axis == 0 else (mod_z, z)
                for way in (0, 1):
                    order = pieces(axis, way, step)
                    if turn < len(order):
                        h = order[turn]
                        origin = mod(at - step if way == 0 else at + step)
                        drain(piece(axis, origin, h), ring_recv.at[axis, way, step - 1, h])
                        if h in pieces(axis, way, step + 1):
                            ring_copy(axis, way, step + 1, h).start()
                        if turn == len(order) - 1:
                            to_sibling(piece(axis, origin, min(order), len(order)))

    def ring_open(axis):
        for turn in range(cut):
            for way in (0, 1):
                if turn < len(pieces(axis, way, 1)):
                    ring_copy(axis, way, 1, pieces(axis, way, 1)[turn]).start()

    drain(w_all.at[pa, y], w1_recv.at[0])
    ring_open(0)
    drain(w_all.at[pb, :, z], w1_recv.at[1])
    ring_open(1)
    to_sibling(w_all.at[pa, y])
    to_sibling(w_all.at[pb, :, z])

    lax.fori_loop(half, heads // 2, inside, 0)

    drain(r1, s1_recv)
    total = r1[0].astype(F32)
    for i in range(1, nz):
        total = total + r1[i].astype(F32)
    tot[...] = total.astype(BF)
    pltpu.make_async_copy(tot, r2.at[y], s2_recv).start()

    def phase2(i, _):
        yy = lax.rem(y + i, ny)
        remote(tot, r2.at[y], s2_send, s2_recv, seq(yy, z, c)).start()
        return 0

    lax.fori_loop(1, ny, phase2, 0)

    ring_step(1)

    drain(r2, s2_recv)
    run = jnp.zeros(total.shape, F32)
    for yy in range(ny):
        run = run + jnp.where(yy < y, r2[yy].astype(F32), 0.0)
    for i in range(nz):
        p_out[i] = run.astype(BF)
        if i < nz - 1:
            run = run + r1[i].astype(F32)
    pltpu.make_async_copy(p_out.at[z], r3.at[z], s3_recv).start()

    def phase3(i, _):
        to = lax.rem(z + i, nz)
        remote(p_out.at[to], r3.at[z], s3_send, s3_recv, seq(y, to, c)).start()
        return 0

    lax.fori_loop(1, nz, phase3, 0)

    ring_step(2)

    drain(r3, s3_recv)
    for i in range(hh):
        chip = r3[i].astype(F32)
        theirs = chip + jnp.where(first_core, s_loc[own + i].astype(F32), 0.0)
        s_pair_out[i] = theirs.astype(BF)
    remote(s_pair_out, prefix.at[pl.ds(own, hh)], s4_send, s4_recv, sib).start()
    for i in range(hh):
        chip = r3[i].astype(F32)
        mine = chip + jnp.where(first_core, 0.0, s_sib[i].astype(F32))
        prefix[own + i] = mine.astype(BF)

    ring_step(3)

    position = me * length + lax.broadcasted_iota(jnp.int32, (length, 1), 0)
    scaling = lax.rsqrt((position.astype(F32) + 1.0) * dk)

    def before(p):
        past = prefix[pl.ds(2 * p, 2)].reshape(2 * dk, dv)
        earlier = dot(two_heads(p), past)
        for h in range(2):
            cols = pl.ds(pl.multiple_of((2 * p + h) * dv, dv), dv)
            attended[:, cols] = (
                (intra[:, cols] + earlier[h * length : (h + 1) * length]) * scaling
            ).astype(BF)

    for p in range(hh // 2):
        before(own // 2 + p)
    drain(prefix.at[pl.ds(other, hh)], s4_recv)
    for p in range(hh // 2):
        before(other // 2 + p)

    for step in range(4, max(ny, nz) // 2 + 1):
        ring_step(step)

    def project(part):
        cols = pl.ds(pl.multiple_of(part * quarter, quarter), quarter)
        return dot(attended[:, cols], w_all[part].reshape(width, quarter), ((1,), (1,)))

    projected = project(pa) + project(pb)
    drain(w_all.at[pl.ds(2 * (1 - c), 2)], sib_recv)
    projected = projected + (project(2 * (1 - c)) + project(2 * (1 - c) + 1))
    hidden = (res_ref[...].astype(F32) + projected).astype(BF)
    hidden_float = hidden.astype(F32)
    intra[:, :width] = hidden_float
    normed = (
        hidden_float
        * lax.rsqrt(jnp.mean(hidden_float * hidden_float, axis=-1, keepdims=True) + 1e-06)
    ).astype(BF)
    xb[...] = dot(spread, normed).astype(BF).reshape(n, CAP, width)

    def offset(i):
        j = lax.rem(i * 37, n)
        return j // row, lax.rem(j // 2, nz), lax.rem(j, 2)

    def ahead(i):
        dy, dz, dc = offset(i)
        return seq(lax.rem(y + dy, ny), lax.rem(z + dz, nz), lax.rem(c + dc, 2))

    def behind(i):
        dy, dz, dc = offset(i)
        return seq(lax.rem(y - dy + ny, ny), lax.rem(z - dz + nz, nz), lax.rem(c - dc + 2, 2))

    per = n // GROUPS
    pl.semaphore_wait(met, ny - 1)
    pltpu.make_async_copy(xb.at[me], xr.at[0], x_recv.at[0]).start()

    def dispatch(i, _):
        to = ahead(i)
        remote(xb.at[to], xr.at[i], x_send, x_recv.at[i // per], to).start()
        return 0

    lax.fori_loop(1, n, dispatch, 0)

    loads[7].wait()
    loads[8].wait()

    def expert(g):
        lo = g * per
        drain(xr.at[pl.ds(lo, per)], x_recv.at[g])
        x = xr[pl.ds(lo, per)].reshape(per * CAP, width)
        act = dot(x, win[...])
        gate, up = act[:, :he], act[:, he:]
        inner = (gate / (1.0 + jnp.exp(-gate)) * up).astype(BF)
        yb[pl.ds(lo, per)] = dot(inner, wout[...]).astype(BF).reshape(per, CAP, width)

    def give_back(i, _):
        to = behind(i)
        remote(yb.at[i], ret.at[me], y_send, y_recv, to).start()
        return 0

    expert(0)
    pltpu.make_async_copy(yb.at[0], ret.at[me], y_recv).start()
    lax.fori_loop(1, per, give_back, 0)

    def group(g, _):
        expert(g)
        lax.fori_loop(g * per, (g + 1) * per, give_back, 0)
        return 0

    lax.fori_loop(1, GROUPS, group, 0)

    r_lane = lax.broadcasted_iota(jnp.int32, (length, rows), 1).astype(F32)
    picks = jnp.concatenate(
        [jnp.where(r_lane == place_col[j], 1.0, 0.0).astype(BF) for j in range(TOP)], axis=0
    )
    drain(ret, y_recv)
    back = ret[...].reshape(rows, width)
    picked = dot(picks, back)
    combined = picked[:length] * gate_col[0] + picked[length:] * gate_col[1]
    o_ref[...] = (intra[:, :width] + combined).astype(BF)

    drain(s_sib, s0_send)
    drain(r1.at[pl.ds(0, nz - 1)], s1_send)
    drain(r2.at[pl.ds(0, ny - 1)], s2_send)
    drain(r3.at[pl.ds(0, nz - 1)], s3_send)
    drain(s_sib, s4_send)
    drain(w_all.at[0, 0, pl.ds(0, nz - 1)], w1_send.at[0])
    drain(w_loc.at[0], w1_send.at[0])
    drain(w_all.at[0, pl.ds(0, ny - 1), 0], w1_send.at[1])
    drain(w_loc.at[0], w1_send.at[1])
    for axis in (0, 1):
        for step in range(1, max(ny, nz) // 2 + 1):
            for way in (0, 1):
                for h in pieces(axis, way, step):
                    ring_copy(axis, way, step, h).wait_send()
    drain(w_all.at[pl.ds(2 * c, 2)], sib_send)
    drain(xb.at[pl.ds(0, n - 1)], x_send)
    drain(yb.at[pl.ds(0, n - 1)], y_send)


def layer(ny, nz, heads, dk, dv, q, k, v, res, wt, w_in, w_out, ids, gates):
    n = ny * nz * 2
    length, width = res.shape
    cols = wt.shape[0]
    quarter = heads * dv // 4
    vmem = pl.BlockSpec(memory_space=pltpu.VMEM)
    hbm = pl.BlockSpec(memory_space=pl.ANY)
    steps = max(ny, nz) // 2
    dma = pltpu.SemaphoreType.DMA
    rows = (n, CAP, width)
    return pl.pallas_call(
        functools.partial(layer_kernel, ny, nz, heads, dk, dv),
        out_shape=jax.ShapeDtypeStruct((length, width), BF),
        in_specs=[hbm] * 9,
        out_specs=vmem,
        scratch_shapes=[
            *[pltpu.VMEM(a.shape, a.dtype) for a in (q, k, v, res, wt, ids, gates)],
            pltpu.VMEM((heads, dk, dv), BF),
            pltpu.VMEM((nz, dk, dv), BF),
            pltpu.VMEM((nz, dk, dv), BF),
            pltpu.VMEM((nz, dk, dv), BF),
            pltpu.VMEM((dk, dv), BF),
            pltpu.VMEM((nz, dk, dv), BF),
            pltpu.VMEM((nz, dk, dv), BF),
            pltpu.VMEM((ny, dk, dv), BF),
            pltpu.VMEM((nz, dk, dv), BF),
            pltpu.VMEM((heads, dk, dv), BF),
            pltpu.VMEM((4, cols, quarter), BF),
            pltpu.VMEM((4, ny, nz, 2, cols, quarter), BF),
            pltpu.VMEM((length, heads * dv), F32),
            pltpu.VMEM((length, heads * dv), BF),
            pltpu.VMEM(w_in.shape, BF),
            pltpu.VMEM(w_out.shape, BF),
            pltpu.VMEM(rows, BF),
            pltpu.VMEM(rows, BF),
            pltpu.VMEM(rows, BF),
            pltpu.VMEM(rows, BF),
            *[dma] * 10,
            dma((2,)),
            dma((2,)),
            pltpu.SemaphoreType.REGULAR,
            dma((2, 2, steps, 4)),
            dma((2, 2, steps, 4)),
            dma,
            dma,
            dma,
            dma((GROUPS,)),
            dma,
            dma,
            dma((9,)),
        ],
        compiler_params=pltpu.CompilerParams(
            collective_id=0, has_side_effects=True, vmem_limit_bytes=60 * 2**20
        ),
        name="layer",
    )(q, k, v, res, wt, w_in, w_out, ids, gates)


def solution(mesh, ny=8, nz=8, heads=16, dk=64, dv=128):
    def per_device(q, k, v, res, w, w_in, w_out, ids, gates):
        return layer(
            ny, nz, heads, dk, dv, q, k, v, res, w.T, w_in[0], w_out[0], ids.T, gates.T
        )

    tokens = P(("win", "seq"), None)
    experts = P("seq", None, None)
    return jax.shard_map(
        per_device,
        mesh=mesh,
        in_specs=(tokens,) * 4 + (P(None, "seq"), experts, experts, tokens, tokens),
        out_specs=tokens,
        check_vma=False,
    )
```

```python
import functools

import jax
import jax.numpy as jnp
from jax import lax
from jax.experimental import pallas as pl
from jax.experimental.pallas import tpu as pltpu
from jax.sharding import PartitionSpec as P

TOP = 2
CAP = 4
GROUPS = 4
MESH = pl.DeviceIdType.MESH
BF = jnp.bfloat16
F32 = jnp.float32


def dot(a, b, dims=((1,), (0,))):
    return lax.dot_general(a, b, (dims, ((), ())), preferred_element_type=F32)


def layer_kernel(
    ny,
    nz,
    heads,
    dk,
    dv,
    q_hbm,
    k_hbm,
    v_hbm,
    res_hbm,
    wt_hbm,
    win_hbm,
    wout_hbm,
    ids_hbm,
    gates_hbm,
    o_ref,
    q_ref,
    k_ref,
    v_ref,
    res_ref,
    wt_ref,
    ids_ref,
    gates_ref,
    s_loc,
    s_sib,
    s_pair,
    s_pair_out,
    tot,
    p_out,
    r1,
    r2,
    r3,
    prefix,
    w_loc,
    w_all,
    intra,
    attended,
    win,
    wout,
    spread,
    xb,
    xr,
    yb,
    ret,
    s0_send,
    s0_recv,
    s1_send,
    s1_recv,
    s2_send,
    s2_recv,
    s3_send,
    s3_recv,
    s4_send,
    s4_recv,
    w1_send,
    w1_recv,
    met,
    ring_send,
    ring_recv,
    sib_send,
    sib_recv,
    x_send,
    x_recv,
    y_send,
    y_recv,
    win_sem,
):
    n = ny * nz * 2
    row = nz * 2
    length = q_ref.shape[0]
    width = res_ref.shape[1]
    he = wout.shape[0]
    part = w_loc.shape[2]
    cut = min(4, nz)
    me = lax.axis_index("seq")
    y, z, c = me // row, lax.rem(me // 2, nz), lax.rem(me, 2)
    at_row = lax.rem(me, row)

    def seq(yy, zz, cc):
        return yy * row + zz * 2 + cc

    def remote(src, dst, ssem, rsem, dev):
        return pltpu.make_async_remote_copy(
            src_ref=src,
            dst_ref=dst,
            send_sem=ssem,
            recv_sem=rsem,
            device_id={"seq": dev},
            device_id_type=MESH,
        )

    def drain(ref, sem):
        pltpu.make_async_copy(ref, ref, sem).wait()

    loads = [
        pltpu.make_async_copy(src, dst, win_sem.at[i])
        for i, (src, dst) in enumerate(
            (
                (k_hbm, k_ref),
                (v_hbm, v_ref),
                (wt_hbm, wt_ref),
                (q_hbm, q_ref),
                (ids_hbm, ids_ref),
                (gates_hbm, gates_ref),
                (res_hbm, res_ref),
                (win_hbm, win),
                (wout_hbm, wout),
            )
        )
    ]
    for load in loads:
        load.start()
    barrier = pltpu.get_barrier_semaphore()

    def greet(dev):
        pl.semaphore_signal(barrier, inc=1, device_id={"seq": dev}, device_id_type=MESH)

    def greet_row(i, _):
        greet(y * row + lax.rem(at_row + i, row))
        return 0

    def greet_column(i, _):
        greet(seq(lax.rem(y + i // 2, ny), z, lax.rem(c + i, 2)))
        return 0

    sib = seq(y, z, 1 - c)
    lax.fori_loop(1, row, greet_row, 0)
    lax.fori_loop(2, 2 * ny, greet_column, 0)

    loads[2].wait()
    for h in range(2):
        w_loc[h] = wt_ref[:, h * part : (h + 1) * part]
    pl.semaphore_wait(barrier, row + 2 * ny - 3)

    ring_at = y + c * (z - y)

    def along_z(i, _):
        to = lax.rem(z + i, nz)
        remote(w_loc.at[0], w_all.at[0, y, z, c], w1_send, w1_recv, seq(y, to, 0)).start()
        return 0

    def along_y(i, _):
        to = lax.rem(y + i, ny)
        remote(w_loc.at[1], w_all.at[1, z, y, c], w1_send, w1_recv, seq(to, z, 1)).start()
        return 0

    pltpu.make_async_copy(
        w_loc.at[c], w_all.at[c, ring_at, y + z - ring_at, c], w1_recv
    ).start()
    lax.fori_loop(1 - c, nz, along_z, 0)
    lax.fori_loop(c, ny, along_y, 0)
    loads[0].wait()
    loads[1].wait()

    for p in range(heads // 2):
        kp = k_ref[:, 2 * p * dk : 2 * (p + 1) * dk]
        kv = dot(kp, v_ref[:, 2 * p * dv : 2 * (p + 1) * dv], ((0,), (0,)))
        s_loc[2 * p] = kv[:dk, :dv].astype(BF)
        s_loc[2 * p + 1] = kv[dk:, dv:].astype(BF)

    hh = heads // 2
    own, other = c * hh, (1 - c) * hh
    first_core = c == 0
    remote(s_loc.at[pl.ds(other, hh)], s_sib, s0_send, s0_recv, sib).start()

    def tell(cc, yy):
        pl.semaphore_signal(
            met, inc=1, device_id={"seq": seq(yy, z, cc)}, device_id_type=MESH
        )

    def tell_column(i, _):
        tell(c, lax.rem(y + i, ny))
        return 0

    lax.fori_loop(1, ny, tell_column, 0)

    eye = lax.broadcasted_iota(jnp.int32, (length, length), 0) == lax.broadcasted_iota(
        jnp.int32, (length, length), 1
    )
    below = lax.broadcasted_iota(jnp.int32, (length, length), 1) < lax.broadcasted_iota(
        jnp.int32, (length, length), 0
    )
    above = lax.broadcasted_iota(jnp.int32, (length, length), 0) < lax.broadcasted_iota(
        jnp.int32, (length, length), 1
    )

    for load in loads[4:7]:
        load.wait()

    def column(r):
        return jnp.sum(jnp.where(eye, r, 0.0), axis=1, keepdims=True)

    def turn_of(e):
        dy = ((e >> (row.bit_length() - 1)) + (ny - y)) & (ny - 1)
        dz = ((e >> 1) + (nz - z)) & (nz - 1)
        dc = (e + c) & 1
        return ((dy * row + dz * 2 + dc) * 45) & (n - 1)

    id_row = [turn_of(ids_ref[j : j + 1, :]).astype(F32) for j in range(TOP)]
    id_col = [column(r) for r in id_row]
    gate_col = [column(gates_ref[j : j + 1, :]) for j in range(TOP)]
    place_row, place_col = [], []
    for j in range(TOP):
        row_count, col_count = 0.0, 0.0
        for i in range(TOP):
            row_count = row_count + jnp.where(above & (id_col[i] == id_row[j]), 1.0, 0.0)
            col_count = col_count + jnp.where(below & (id_col[j] == id_row[i]), 1.0, 0.0)
        place_row.append(id_row[j] * CAP + jnp.sum(row_count, axis=0, keepdims=True))
        place_col.append(id_col[j] * CAP + jnp.sum(col_count, axis=1, keepdims=True))
    rows = n * CAP
    r_iota = lax.broadcasted_iota(jnp.int32, (rows, length), 0).astype(F32)
    spread[...] = jnp.where(
        (r_iota == place_row[0]) | (r_iota == place_row[1]), 1.0, 0.0
    ).astype(BF)

    drain(s_sib, s0_recv)
    for i in range(hh):
        both = s_loc[own + i].astype(F32) + s_sib[i].astype(F32)
        s_pair[i] = both.astype(BF)
    pltpu.make_async_copy(s_pair.at[z], r1.at[z], s1_recv).start()

    def phase1(i, _):
        to = lax.rem(z + i, nz)
        remote(s_pair.at[to], r1.at[z], s1_send, s1_recv, seq(y, to, c)).start()
        return 0

    lax.fori_loop(1, nz, phase1, 0)

    t_row = lax.broadcasted_iota(jnp.int32, (2 * length, length), 0)
    t_col = lax.broadcasted_iota(jnp.int32, (2 * length, length), 1)
    causal = lax.rem(t_row, length) >= t_col
    first = lax.broadcasted_iota(jnp.int32, (length, 2 * dk), 1) < dk

    def two_heads(p):
        qp = q_ref[:, pl.ds(pl.multiple_of(p * 2 * dk, 2 * dk), 2 * dk)]
        zero = jnp.zeros_like(qp)
        return jnp.concatenate(
            [jnp.where(first, qp, zero), jnp.where(first, zero, qp)], axis=0
        )

    def inside(p, _):
        kp = k_ref[:, pl.ds(pl.multiple_of(p * 2 * dk, 2 * dk), 2 * dk)]
        at = pl.multiple_of(p * 2 * dv, 2 * dv)
        scores = dot(two_heads(p), kp, ((1,), (1,)))
        scores = jnp.where(causal, scores, 0.0).astype(BF)
        vp = v_ref[:, pl.ds(at, 2 * dv)]
        intra[:, pl.ds(at, dv)] = dot(scores[:length], vp[:, :dv])
        intra[:, pl.ds(pl.multiple_of(at + dv, dv), dv)] = dot(scores[length:], vp[:, dv:])
        return 0

    loads[3].wait()
    half = heads // 4
    lax.fori_loop(0, half, inside, 0)

    def around(v):
        return lax.rem(v + 2 * nz, nz)

    def piece(origin, h, many=1):
        return w_all.at[c, origin, pl.ds(h * (nz // cut), many * (nz // cut))]

    def pieces(way, step):
        mine = tuple(range(way * cut // 2, (way + 1) * cut // 2))
        if 2 * step > nz:
            return ()
        return mine if 2 * step == nz else mine + tuple(set(range(cut)) - set(mine))

    def to_sibling(ref):
        remote(ref, ref, sib_send, sib_recv, sib).start()

    def ring_copy(way, step, h):
        sign = 1 if way == 0 else -1
        ref = piece(around(ring_at - sign * (step - 1)), h)
        to = around(ring_at + sign)
        dev = seq(to + c * (y - to), z + c * (to - z), c)
        place = (way, step - 1, h)
        return remote(ref, ref, ring_send.at[place], ring_recv.at[place], dev)

    def ring_step(step):
        for turn in range(cut):
            for way in (0, 1):
                order = pieces(way, step)
                if turn < len(order):
                    h = order[turn]
                    origin = around(ring_at - step if way == 0 else ring_at + step)
                    drain(piece(origin, h), ring_recv.at[way, step - 1, h])
                    if h in pieces(way, step + 1):
                        ring_copy(way, step + 1, h).start()
                    if turn == len(order) - 1:
                        to_sibling(piece(origin, min(order), len(order)))

    drain(w_all.at[c, ring_at], w1_recv)
    for turn in range(cut):
        for way in (0, 1):
            if turn < len(pieces(way, 1)):
                ring_copy(way, 1, pieces(way, 1)[turn]).start()
    to_sibling(w_all.at[c, ring_at])

    lax.fori_loop(half, heads // 2, inside, 0)

    drain(r1, s1_recv)
    total = r1[0].astype(F32)
    for i in range(1, nz):
        total = total + r1[i].astype(F32)
    tot[...] = total.astype(BF)
    pltpu.make_async_copy(tot, r2.at[y], s2_recv).start()

    def phase2(i, _):
        yy = lax.rem(y + i, ny)
        remote(tot, r2.at[y], s2_send, s2_recv, seq(yy, z, c)).start()
        return 0

    lax.fori_loop(1, ny, phase2, 0)

    ring_step(1)

    drain(r2, s2_recv)
    run = jnp.zeros(total.shape, F32)
    for yy in range(ny):
        run = run + jnp.where(yy < y, r2[yy].astype(F32), 0.0)
    for i in range(nz):
        p_out[i] = run.astype(BF)
        if i < nz - 1:
            run = run + r1[i].astype(F32)
    pltpu.make_async_copy(p_out.at[z], r3.at[z], s3_recv).start()

    def phase3(i, _):
        to = lax.rem(z + i, nz)
        remote(p_out.at[to], r3.at[z], s3_send, s3_recv, seq(y, to, c)).start()
        return 0

    lax.fori_loop(1, nz, phase3, 0)

    ring_step(2)

    drain(r3, s3_recv)
    for i in range(hh):
        chip = r3[i].astype(F32)
        theirs = chip + jnp.where(first_core, s_loc[own + i].astype(F32), 0.0)
        s_pair_out[i] = theirs.astype(BF)
    remote(s_pair_out, prefix.at[pl.ds(own, hh)], s4_send, s4_recv, sib).start()
    for i in range(hh):
        chip = r3[i].astype(F32)
        mine = chip + jnp.where(first_core, 0.0, s_sib[i].astype(F32))
        prefix[own + i] = mine.astype(BF)

    ring_step(3)

    position = me * length + lax.broadcasted_iota(jnp.int32, (length, 1), 0)
    scaling = lax.rsqrt((position.astype(F32) + 1.0) * dk)

    def before(p):
        past = prefix[pl.ds(2 * p, 2)].reshape(2 * dk, dv)
        earlier = dot(two_heads(p), past)
        for h in range(2):
            cols = pl.ds(pl.multiple_of((2 * p + h) * dv, dv), dv)
            attended[:, cols] = (
                (intra[:, cols] + earlier[h * length : (h + 1) * length]) * scaling
            ).astype(BF)

    for p in range(hh // 2):
        before(own // 2 + p)
    drain(prefix.at[pl.ds(other, hh)], s4_recv)
    for p in range(hh // 2):
        before(other // 2 + p)

    for step in range(4, nz // 2 + 1):
        ring_step(step)

    def project(h, add):
        att = attended[:, h * part : (h + 1) * part]
        rows_of = width // ny
        for yy in range(ny):
            w = w_all[0, yy] if h == 0 else w_all[1, :, yy]
            cols = slice(width + yy * rows_of, width + (yy + 1) * rows_of)
            got = dot(att, w.reshape(rows_of, part), ((1,), (1,)))
            intra[:, cols] = intra[:, cols] + got if add else got

    pl.when(c == 0)(functools.partial(project, 0, False))
    pl.when(c == 1)(functools.partial(project, 1, False))
    drain(w_all.at[1 - c], sib_recv)
    pl.when(c == 0)(functools.partial(project, 1, True))
    pl.when(c == 1)(functools.partial(project, 0, True))
    projected = intra[:, width : 2 * width]
    hidden = (res_ref[...].astype(F32) + projected).astype(BF)
    hidden_float = hidden.astype(F32)
    intra[:, :width] = hidden_float
    normed = (
        hidden_float
        * lax.rsqrt(jnp.mean(hidden_float * hidden_float, axis=-1, keepdims=True) + 1e-06)
    ).astype(BF)

    def offset(i):
        j = lax.rem(i * 37, n)
        return j // row, lax.rem(j // 2, nz), lax.rem(j, 2)

    def ahead(i):
        dy, dz, dc = offset(i)
        return seq(lax.rem(y + dy, ny), lax.rem(z + dz, nz), lax.rem(c + dc, 2))

    def behind(i):
        dy, dz, dc = offset(i)
        return seq(lax.rem(y - dy + ny, ny), lax.rem(z - dz + nz, nz), lax.rem(c - dc + 2, 2))

    per = n // GROUPS
    pl.semaphore_wait(met, ny - 1)

    def fill(g):
        mine = spread[pl.ds(pl.multiple_of(g * per * CAP, per * CAP), per * CAP)]
        xb[pl.ds(g * per, per)] = dot(mine, normed).astype(BF).reshape(per, CAP, width)

    def dispatch(i, _):
        remote(xb.at[i], xr.at[i], x_send, x_recv.at[i // per], ahead(i)).start()
        return 0

    fill(0)
    pltpu.make_async_copy(xb.at[0], xr.at[0], x_recv.at[0]).start()
    lax.fori_loop(1, per, dispatch, 0)
    for g in range(1, GROUPS):
        fill(g)
        lax.fori_loop(g * per, (g + 1) * per, dispatch, 0)

    loads[7].wait()
    loads[8].wait()

    def expert(g):
        lo = g * per
        drain(xr.at[pl.ds(lo, per)], x_recv.at[g])
        x = xr[pl.ds(lo, per)].reshape(per * CAP, width)
        act = dot(x, win[...])
        gate, up = act[:, :he], act[:, he:]
        inner = (gate / (1.0 + jnp.exp(-gate)) * up).astype(BF)
        yb[pl.ds(lo, per)] = dot(inner, wout[...]).astype(BF).reshape(per, CAP, width)

    def give_back(i, _):
        to = behind(i)
        remote(yb.at[i], ret.at[i], y_send, y_recv.at[i // per], to).start()
        return 0

    expert(0)
    pltpu.make_async_copy(yb.at[0], ret.at[0], y_recv.at[0]).start()
    lax.fori_loop(1, per, give_back, 0)

    def group(g, _):
        expert(g)
        lax.fori_loop(g * per, (g + 1) * per, give_back, 0)
        return 0

    lax.fori_loop(1, GROUPS, group, 0)

    wide = per * CAP
    r_lane = lax.broadcasted_iota(jnp.int32, (length, wide), 1).astype(F32)
    combined = jnp.zeros((length, width), F32)
    for g in range(GROUPS):
        picks = jnp.concatenate(
            [
                jnp.where(r_lane + g * wide == place_col[j], 1.0, 0.0).astype(BF)
                for j in range(TOP)
            ],
            axis=0,
        )
        drain(ret.at[pl.ds(g * per, per)], y_recv.at[g])
        picked = dot(picks, ret[g * per : (g + 1) * per].reshape(wide, width))
        combined = combined + (picked[:length] * gate_col[0] + picked[length:] * gate_col[1])
    o_ref[...] = (intra[:, :width] + combined).astype(BF)

    drain(s_sib, s0_send)
    drain(r1.at[pl.ds(0, nz - 1)], s1_send)
    drain(r2.at[pl.ds(0, ny - 1)], s2_send)
    drain(r3.at[pl.ds(0, nz - 1)], s3_send)
    drain(s_sib, s4_send)
    drain(w_all.at[0, 0, pl.ds(0, nz - 1)], w1_send)
    drain(w_loc.at[0], w1_send)
    for step in range(1, nz // 2 + 1):
        for way in (0, 1):
            for h in pieces(way, step):
                ring_copy(way, step, h).wait_send()
    drain(w_all.at[c], sib_send)
    drain(xb.at[pl.ds(0, n - 1)], x_send)
    drain(yb.at[pl.ds(0, n - 1)], y_send)


def layer(ny, nz, heads, dk, dv, q, k, v, res, wt, w_in, w_out, ids, gates):
    n = ny * nz * 2
    length, width = res.shape
    cols = wt.shape[0]
    part = heads * dv // 2
    assert ny == nz
    vmem = pl.BlockSpec(memory_space=pltpu.VMEM)
    hbm = pl.BlockSpec(memory_space=pl.ANY)
    steps = max(ny, nz) // 2
    dma = pltpu.SemaphoreType.DMA
    rows = (n, CAP, width)
    return pl.pallas_call(
        functools.partial(layer_kernel, ny, nz, heads, dk, dv),
        out_shape=jax.ShapeDtypeStruct((length, width), BF),
        in_specs=[hbm] * 9,
        out_specs=vmem,
        scratch_shapes=[
            *[pltpu.VMEM(a.shape, a.dtype) for a in (q, k, v, res, wt, ids, gates)],
            pltpu.VMEM((heads, dk, dv), BF),
            pltpu.VMEM((nz, dk, dv), BF),
            pltpu.VMEM((nz, dk, dv), BF),
            pltpu.VMEM((nz, dk, dv), BF),
            pltpu.VMEM((dk, dv), BF),
            pltpu.VMEM((nz, dk, dv), BF),
            pltpu.VMEM((nz, dk, dv), BF),
            pltpu.VMEM((ny, dk, dv), BF),
            pltpu.VMEM((nz, dk, dv), BF),
            pltpu.VMEM((heads, dk, dv), BF),
            pltpu.VMEM((2, cols, part), BF),
            pltpu.VMEM((2, ny, nz, 2, cols, part), BF),
            pltpu.VMEM((length, heads * dv), F32),
            pltpu.VMEM((length, heads * dv), BF),
            pltpu.VMEM(w_in.shape, BF),
            pltpu.VMEM(w_out.shape, BF),
            pltpu.VMEM((n * CAP, length), BF),
            pltpu.VMEM(rows, BF),
            pltpu.VMEM(rows, BF),
            pltpu.VMEM(rows, BF),
            pltpu.VMEM(rows, BF),
            *[dma] * 12,
            pltpu.SemaphoreType.REGULAR,
            dma((2, steps, 4)),
            dma((2, steps, 4)),
            dma,
            dma,
            dma,
            dma((GROUPS,)),
            dma,
            dma((GROUPS,)),
            dma((9,)),
        ],
        compiler_params=pltpu.CompilerParams(
            collective_id=0, has_side_effects=True, vmem_limit_bytes=60 * 2**20
        ),
        name="layer",
    )(q, k, v, res, wt, w_in, w_out, ids, gates)


def solution(mesh, ny=8, nz=8, heads=16, dk=64, dv=128):
    def per_device(q, k, v, res, w, w_in, w_out, ids, gates):
        return layer(
            ny, nz, heads, dk, dv, q, k, v, res, w.T, w_in[0], w_out[0], ids.T, gates.T
        )

    tokens = P(("win", "seq"), None)
    experts = P("seq", None, None)
    return jax.shard_map(
        per_device,
        mesh=mesh,
        in_specs=(tokens,) * 4 + (P(None, "seq"), experts, experts, tokens, tokens),
        out_specs=tokens,
        check_vma=False,
    )
```

```python
import functools

import jax
import jax.numpy as jnp
from jax import lax
from jax.experimental import pallas as pl
from jax.experimental.pallas import tpu as pltpu
from jax.sharding import PartitionSpec as P

TOP = 2
CAP = 4
GROUPS = 4
MESH = pl.DeviceIdType.MESH
BF = jnp.bfloat16
F32 = jnp.float32


def dot(a, b, dims=((1,), (0,))):
    return lax.dot_general(a, b, (dims, ((), ())), preferred_element_type=F32)


def layer_kernel(
    ny,
    nz,
    heads,
    dk,
    dv,
    q_hbm,
    k_hbm,
    v_hbm,
    res_hbm,
    wt_hbm,
    win_hbm,
    wout_hbm,
    ids_hbm,
    gates_hbm,
    o_ref,
    q_ref,
    k_ref,
    v_ref,
    res_ref,
    wt_ref,
    ids_ref,
    gates_ref,
    s_loc,
    s_sib,
    s_pair,
    s_pair_out,
    tot,
    p_out,
    r1,
    r2,
    r3,
    prefix,
    w_loc,
    w_all,
    intra,
    attended,
    win,
    wout,
    spread,
    xb,
    xr,
    yb,
    ret,
    s0_send,
    s0_recv,
    s1_send,
    s1_recv,
    s2_send,
    s2_recv,
    s3_send,
    s3_recv,
    s4_send,
    s4_recv,
    w1_send,
    w1_recv,
    met,
    ring_send,
    ring_recv,
    sib_send,
    sib_recv,
    x_send,
    x_recv,
    y_send,
    y_recv,
    win_sem,
):
    n = ny * nz * 2
    row = nz * 2
    length = q_ref.shape[0]
    width = res_ref.shape[1]
    he = wout.shape[0]
    quarter = w_loc.shape[2]
    cut = min(4, ny, nz)
    me = lax.axis_index("seq")
    y, z, c = me // row, lax.rem(me // 2, nz), lax.rem(me, 2)
    at_row = lax.rem(me, row)

    def seq(yy, zz, cc):
        return yy * row + zz * 2 + cc

    def remote(src, dst, ssem, rsem, dev):
        return pltpu.make_async_remote_copy(
            src_ref=src,
            dst_ref=dst,
            send_sem=ssem,
            recv_sem=rsem,
            device_id={"seq": dev},
            device_id_type=MESH,
        )

    def drain(ref, sem):
        pltpu.make_async_copy(ref, ref, sem).wait()

    loads = [
        pltpu.make_async_copy(src, dst, win_sem.at[i])
        for i, (src, dst) in enumerate(
            (
                (k_hbm, k_ref),
                (v_hbm, v_ref),
                (wt_hbm, wt_ref),
                (q_hbm, q_ref),
                (ids_hbm, ids_ref),
                (gates_hbm, gates_ref),
                (res_hbm, res_ref),
                (win_hbm, win),
                (wout_hbm, wout),
            )
        )
    ]
    for load in loads:
        load.start()
    barrier = pltpu.get_barrier_semaphore()

    def greet(dev):
        pl.semaphore_signal(barrier, inc=1, device_id={"seq": dev}, device_id_type=MESH)

    def greet_row(i, _):
        greet(y * row + lax.rem(at_row + i, row))
        return 0

    def greet_column(i, _):
        greet(seq(lax.rem(y + i // 2, ny), z, lax.rem(c + i, 2)))
        return 0

    sib = seq(y, z, 1 - c)
    lax.fori_loop(1, row, greet_row, 0)
    lax.fori_loop(2, 2 * ny, greet_column, 0)

    loads[2].wait()
    for part in range(4):
        w_loc[part] = wt_ref[:, part * quarter : (part + 1) * quarter]
    pl.semaphore_wait(barrier, row + 2 * ny - 3)

    pa, pb = 2 * c, 2 * c + 1

    def keep(part, sem):
        pltpu.make_async_copy(w_loc.at[part], w_all.at[part, y, z, c], sem).start()

    def along_z(i, _):
        to = lax.rem(at_row + i, row)
        part = 2 * lax.rem(to, 2)
        remote(
            w_loc.at[part], w_all.at[part, y, z, c], w1_send.at[0], w1_recv.at[0], y * row + to
        ).start()
        return 0

    def along_y(i, _):
        cc = lax.rem(c + i, 2)
        part = 2 * cc + 1
        remote(
            w_loc.at[part],
            w_all.at[part, y, z, c],
            w1_send.at[1],
            w1_recv.at[1],
            seq(lax.rem(y + i // 2, ny), z, cc),
        ).start()
        return 0

    keep(pa, w1_recv.at[0])
    keep(pb, w1_recv.at[1])
    lax.fori_loop(1, row, along_z, 0)
    lax.fori_loop(1, 2 * ny, along_y, 0)

    loads[0].wait()
    loads[1].wait()

    for p in range(heads // 2):
        kp = k_ref[:, 2 * p * dk : 2 * (p + 1) * dk]
        kv = dot(kp, v_ref[:, 2 * p * dv : 2 * (p + 1) * dv], ((0,), (0,)))
        s_loc[2 * p] = kv[:dk, :dv].astype(BF)
        s_loc[2 * p + 1] = kv[dk:, dv:].astype(BF)

    hh = heads // 2
    own, other = c * hh, (1 - c) * hh
    first_core = c == 0
    remote(s_loc.at[pl.ds(other, hh)], s_sib, s0_send, s0_recv, sib).start()

    def tell(cc, yy):
        pl.semaphore_signal(
            met, inc=1, device_id={"seq": seq(yy, z, cc)}, device_id_type=MESH
        )

    def tell_column(i, _):
        tell(c, lax.rem(y + i, ny))
        return 0

    lax.fori_loop(1, ny, tell_column, 0)

    eye = lax.broadcasted_iota(jnp.int32, (length, length), 0) == lax.broadcasted_iota(
        jnp.int32, (length, length), 1
    )
    below = lax.broadcasted_iota(jnp.int32, (length, length), 1) < lax.broadcasted_iota(
        jnp.int32, (length, length), 0
    )
    above = lax.broadcasted_iota(jnp.int32, (length, length), 0) < lax.broadcasted_iota(
        jnp.int32, (length, length), 1
    )

    for load in loads[4:7]:
        load.wait()

    def column(r):
        return jnp.sum(jnp.where(eye, r, 0.0), axis=1, keepdims=True)

    def turn_of(e):
        dy = ((e >> (row.bit_length() - 1)) + (ny - y)) & (ny - 1)
        dz = ((e >> 1) + (nz - z)) & (nz - 1)
        dc = (e + c) & 1
        return ((dy * row + dz * 2 + dc) * 45) & (n - 1)

    id_row = [turn_of(ids_ref[j : j + 1, :]).astype(F32) for j in range(TOP)]
    id_col = [column(r) for r in id_row]
    gate_col = [column(gates_ref[j : j + 1, :]) for j in range(TOP)]
    place_row, place_col = [], []
    for j in range(TOP):
        row_count, col_count = 0.0, 0.0
        for i in range(TOP):
            row_count = row_count + jnp.where(above & (id_col[i] == id_row[j]), 1.0, 0.0)
            col_count = col_count + jnp.where(below & (id_col[j] == id_row[i]), 1.0, 0.0)
        place_row.append(id_row[j] * CAP + jnp.sum(row_count, axis=0, keepdims=True))
        place_col.append(id_col[j] * CAP + jnp.sum(col_count, axis=1, keepdims=True))
    rows = n * CAP
    r_iota = lax.broadcasted_iota(jnp.int32, (rows, length), 0).astype(F32)
    spread[...] = jnp.where(
        (r_iota == place_row[0]) | (r_iota == place_row[1]), 1.0, 0.0
    ).astype(BF)

    drain(s_sib, s0_recv)
    for i in range(hh):
        both = s_loc[own + i].astype(F32) + s_sib[i].astype(F32)
        s_pair[i] = both.astype(BF)
    pltpu.make_async_copy(s_pair.at[z], r1.at[z], s1_recv).start()

    def far_first(i, size):
        return size // 2 + (1 - 2 * lax.rem(i, 2)) * (i // 2) + size

    def phase1(i, _):
        to = lax.rem(z + far_first(i, nz), nz)
        remote(s_pair.at[to], r1.at[z], s1_send, s1_recv, seq(y, to, c)).start()
        return 0

    lax.fori_loop(1, nz, phase1, 0)

    t_row = lax.broadcasted_iota(jnp.int32, (2 * length, length), 0)
    t_col = lax.broadcasted_iota(jnp.int32, (2 * length, length), 1)
    causal = lax.rem(t_row, length) >= t_col
    first = lax.broadcasted_iota(jnp.int32, (length, 2 * dk), 1) < dk

    def two_heads(p):
        qp = q_ref[:, pl.ds(pl.multiple_of(p * 2 * dk, 2 * dk), 2 * dk)]
        zero = jnp.zeros_like(qp)
        return jnp.concatenate(
            [jnp.where(first, qp, zero), jnp.where(first, zero, qp)], axis=0
        )

    def inside(p, _):
        kp = k_ref[:, pl.ds(pl.multiple_of(p * 2 * dk, 2 * dk), 2 * dk)]
        at = pl.multiple_of(p * 2 * dv, 2 * dv)
        scores = dot(two_heads(p), kp, ((1,), (1,)))
        scores = jnp.where(causal, scores, 0.0).astype(BF)
        vp = v_ref[:, pl.ds(at, 2 * dv)]
        intra[:, pl.ds(at, dv)] = dot(scores[:length], vp[:, :dv])
        intra[:, pl.ds(pl.multiple_of(at + dv, dv), dv)] = dot(scores[length:], vp[:, dv:])
        return 0

    loads[3].wait()
    half = heads // 4
    lax.fori_loop(0, half, inside, 0)

    def mod_y(v):
        return lax.rem(v + 2 * ny, ny)

    def mod_z(v):
        return lax.rem(v + 2 * nz, nz)

    def piece(axis, origin, h, many=1):
        if axis == 0:
            return w_all.at[pa, origin, pl.ds(h * (nz // cut), many * (nz // cut))]
        return w_all.at[pb, pl.ds(h * (ny // cut), many * (ny // cut)), origin]

    def pieces(axis, way, step):
        size = ny if axis == 0 else nz
        mine = tuple(range(way * cut // 2, (way + 1) * cut // 2))
        if 2 * step > size:
            return ()
        return mine if 2 * step == size else mine + tuple(set(range(cut)) - set(mine))

    def to_sibling(ref):
        remote(ref, ref, sib_send, sib_recv, sib).start()

    def ring_copy(axis, way, step, h):
        mod, at = (mod_y, y) if axis == 0 else (mod_z, z)
        sign = 1 if way == 0 else -1
        ref = piece(axis, mod(at - sign * (step - 1)), h)
        dev = seq(mod(at + sign), z, c) if axis == 0 else seq(y, mod(at + sign), c)
        place = (axis, way, step - 1, h)
        return remote(ref, ref, ring_send.at[place], ring_recv.at[place], dev)

    def ring_step(step):
        for turn in range(cut):
            for axis in (0, 1):
                mod, at = (mod_y, y) if axis == 0 else (mod_z, z)
                for way in (0, 1):
                    order = pieces(axis, way, step)
                    if turn < len(order):
                        h = order[turn]
                        origin = mod(at - step if way == 0 else at + step)
                        drain(piece(axis, origin, h), ring_recv.at[axis, way, step - 1, h])
                        if h in pieces(axis, way, step + 1):
                            ring_copy(axis, way, step + 1, h).start()
                        if turn == len(order) - 1:
                            to_sibling(piece(axis, origin, min(order), len(order)))

    def ring_open(axis):
        for turn in range(cut):
            for way in (0, 1):
                if turn < len(pieces(axis, way, 1)):
                    ring_copy(axis, way, 1, pieces(axis, way, 1)[turn]).start()

    drain(w_all.at[pa, y], w1_recv.at[0])
    ring_open(0)
    drain(w_all.at[pb, :, z], w1_recv.at[1])
    ring_open(1)
    to_sibling(w_all.at[pa, y])
    to_sibling(w_all.at[pb, :, z])

    lax.fori_loop(half, heads // 2, inside, 0)

    drain(r1, s1_recv)
    total = r1[0].astype(F32)
    for i in range(1, nz):
        total = total + r1[i].astype(F32)
    tot[...] = total.astype(BF)
    pltpu.make_async_copy(tot, r2.at[y], s2_recv).start()

    def phase2(i, _):
        yy = lax.rem(y + far_first(i, ny), ny)
        remote(tot, r2.at[y], s2_send, s2_recv, seq(yy, z, c)).start()
        return 0

    lax.fori_loop(1, ny, phase2, 0)

    ring_step(1)

    drain(r2, s2_recv)
    run = jnp.zeros(total.shape, F32)
    for yy in range(ny):
        run = run + jnp.where(yy < y, r2[yy].astype(F32), 0.0)
    for i in range(nz):
        p_out[i] = run.astype(BF)
        if i < nz - 1:
            run = run + r1[i].astype(F32)
    pltpu.make_async_copy(p_out.at[z], r3.at[z], s3_recv).start()

    def phase3(i, _):
        to = lax.rem(z + far_first(i, nz), nz)
        remote(p_out.at[to], r3.at[z], s3_send, s3_recv, seq(y, to, c)).start()
        return 0

    lax.fori_loop(1, nz, phase3, 0)

    ring_step(2)

    drain(r3, s3_recv)
    for i in range(hh):
        chip = r3[i].astype(F32)
        theirs = chip + jnp.where(first_core, s_loc[own + i].astype(F32), 0.0)
        s_pair_out[i] = theirs.astype(BF)
    remote(s_pair_out, prefix.at[pl.ds(own, hh)], s4_send, s4_recv, sib).start()
    for i in range(hh):
        chip = r3[i].astype(F32)
        mine = chip + jnp.where(first_core, 0.0, s_sib[i].astype(F32))
        prefix[own + i] = mine.astype(BF)

    ring_step(3)

    position = me * length + lax.broadcasted_iota(jnp.int32, (length, 1), 0)
    scaling = lax.rsqrt((position.astype(F32) + 1.0) * dk)

    def before(p):
        past = prefix[pl.ds(2 * p, 2)].reshape(2 * dk, dv)
        earlier = dot(two_heads(p), past)
        for h in range(2):
            cols = pl.ds(pl.multiple_of((2 * p + h) * dv, dv), dv)
            attended[:, cols] = (
                (intra[:, cols] + earlier[h * length : (h + 1) * length]) * scaling
            ).astype(BF)

    for p in range(hh // 2):
        before(own // 2 + p)
    drain(prefix.at[pl.ds(other, hh)], s4_recv)
    for p in range(hh // 2):
        before(other // 2 + p)

    for step in range(4, max(ny, nz) // 2 + 1):
        ring_step(step)

    def project(part):
        cols = pl.ds(pl.multiple_of(part * quarter, quarter), quarter)
        return dot(attended[:, cols], w_all[part].reshape(width, quarter), ((1,), (1,)))

    projected = project(pa) + project(pb)
    drain(w_all.at[pl.ds(2 * (1 - c), 2)], sib_recv)
    projected = projected + (project(2 * (1 - c)) + project(2 * (1 - c) + 1))
    hidden = (res_ref[...].astype(F32) + projected).astype(BF)
    hidden_float = hidden.astype(F32)
    intra[:, :width] = hidden_float
    normed = (
        hidden_float
        * lax.rsqrt(jnp.mean(hidden_float * hidden_float, axis=-1, keepdims=True) + 1e-06)
    ).astype(BF)

    def offset(i):
        j = lax.rem(i * 37, n)
        return j // row, lax.rem(j // 2, nz), lax.rem(j, 2)

    def ahead(i):
        dy, dz, dc = offset(i)
        return seq(lax.rem(y + dy, ny), lax.rem(z + dz, nz), lax.rem(c + dc, 2))

    def behind(i):
        dy, dz, dc = offset(i)
        return seq(lax.rem(y - dy + ny, ny), lax.rem(z - dz + nz, nz), lax.rem(c - dc + 2, 2))

    per = n // GROUPS
    pl.semaphore_wait(met, ny - 1)

    def fill(g):
        mine = spread[pl.ds(pl.multiple_of(g * per * CAP, per * CAP), per * CAP)]
        xb[pl.ds(g * per, per)] = dot(mine, normed).astype(BF).reshape(per, CAP, width)

    def dispatch(i, _):
        remote(xb.at[i], xr.at[i], x_send, x_recv.at[i // per], ahead(i)).start()
        return 0

    fill(0)
    pltpu.make_async_copy(xb.at[0], xr.at[0], x_recv.at[0]).start()
    lax.fori_loop(1, per, dispatch, 0)
    for g in range(1, GROUPS):
        fill(g)
        lax.fori_loop(g * per, (g + 1) * per, dispatch, 0)

    loads[7].wait()
    loads[8].wait()

    def expert(g):
        lo = g * per
        drain(xr.at[pl.ds(lo, per)], x_recv.at[g])
        x = xr[pl.ds(lo, per)].reshape(per * CAP, width)
        act = dot(x, win[...])
        gate, up = act[:, :he], act[:, he:]
        inner = (gate / (1.0 + jnp.exp(-gate)) * up).astype(BF)
        yb[pl.ds(lo, per)] = dot(inner, wout[...]).astype(BF).reshape(per, CAP, width)

    def give_back(i, _):
        to = behind(i)
        remote(yb.at[i], ret.at[i], y_send, y_recv.at[i // per], to).start()
        return 0

    expert(0)
    pltpu.make_async_copy(yb.at[0], ret.at[0], y_recv.at[0]).start()
    lax.fori_loop(1, per, give_back, 0)

    def group(g, _):
        expert(g)
        lax.fori_loop(g * per, (g + 1) * per, give_back, 0)
        return 0

    lax.fori_loop(1, GROUPS, group, 0)

    wide = per * CAP
    r_lane = lax.broadcasted_iota(jnp.int32, (length, wide), 1).astype(F32)
    combined = jnp.zeros((length, width), F32)
    for g in range(GROUPS):
        picks = jnp.concatenate(
            [
                jnp.where(r_lane + g * wide == place_col[j], 1.0, 0.0).astype(BF)
                for j in range(TOP)
            ],
            axis=0,
        )
        drain(ret.at[pl.ds(g * per, per)], y_recv.at[g])
        picked = dot(picks, ret[g * per : (g + 1) * per].reshape(wide, width))
        combined = combined + (picked[:length] * gate_col[0] + picked[length:] * gate_col[1])
    o_ref[...] = (intra[:, :width] + combined).astype(BF)

    drain(s_sib, s0_send)
    drain(r1.at[pl.ds(0, nz - 1)], s1_send)
    drain(r2.at[pl.ds(0, ny - 1)], s2_send)
    drain(r3.at[pl.ds(0, nz - 1)], s3_send)
    drain(s_sib, s4_send)
    drain(w_all.at[0, 0, pl.ds(0, nz - 1)], w1_send.at[0])
    drain(w_loc.at[0], w1_send.at[0])
    drain(w_all.at[0, pl.ds(0, ny - 1), 0], w1_send.at[1])
    drain(w_loc.at[0], w1_send.at[1])
    for axis in (0, 1):
        for step in range(1, max(ny, nz) // 2 + 1):
            for way in (0, 1):
                for h in pieces(axis, way, step):
                    ring_copy(axis, way, step, h).wait_send()
    drain(w_all.at[pl.ds(2 * c, 2)], sib_send)
    drain(xb.at[pl.ds(0, n - 1)], x_send)
    drain(yb.at[pl.ds(0, n - 1)], y_send)


def layer(ny, nz, heads, dk, dv, q, k, v, res, wt, w_in, w_out, ids, gates):
    n = ny * nz * 2
    length, width = res.shape
    cols = wt.shape[0]
    quarter = heads * dv // 4
    vmem = pl.BlockSpec(memory_space=pltpu.VMEM)
    hbm = pl.BlockSpec(memory_space=pl.ANY)
    steps = max(ny, nz) // 2
    dma = pltpu.SemaphoreType.DMA
    rows = (n, CAP, width)
    return pl.pallas_call(
        functools.partial(layer_kernel, ny, nz, heads, dk, dv),
        out_shape=pltpu.VMEM((length, width), BF),
        in_specs=[hbm] * 9,
        out_specs=vmem,
        scratch_shapes=[
            *[pltpu.VMEM(a.shape, a.dtype) for a in (q, k, v, res, wt, ids, gates)],
            pltpu.VMEM((heads, dk, dv), BF),
            pltpu.VMEM((nz, dk, dv), BF),
            pltpu.VMEM((nz, dk, dv), BF),
            pltpu.VMEM((nz, dk, dv), BF),
            pltpu.VMEM((dk, dv), BF),
            pltpu.VMEM((nz, dk, dv), BF),
            pltpu.VMEM((nz, dk, dv), BF),
            pltpu.VMEM((ny, dk, dv), BF),
            pltpu.VMEM((nz, dk, dv), BF),
            pltpu.VMEM((heads, dk, dv), BF),
            pltpu.VMEM((4, cols, quarter), BF),
            pltpu.VMEM((4, ny, nz, 2, cols, quarter), BF),
            pltpu.VMEM((length, heads * dv), F32),
            pltpu.VMEM((length, heads * dv), BF),
            pltpu.VMEM(w_in.shape, BF),
            pltpu.VMEM(w_out.shape, BF),
            pltpu.VMEM((n * CAP, length), BF),
            pltpu.VMEM(rows, BF),
            pltpu.VMEM(rows, BF),
            pltpu.VMEM(rows, BF),
            pltpu.VMEM(rows, BF),
            *[dma] * 10,
            dma((2,)),
            dma((2,)),
            pltpu.SemaphoreType.REGULAR,
            dma((2, 2, steps, 4)),
            dma((2, 2, steps, 4)),
            dma,
            dma,
            dma,
            dma((GROUPS,)),
            dma,
            dma((GROUPS,)),
            dma((9,)),
        ],
        compiler_params=pltpu.CompilerParams(
            collective_id=0, has_side_effects=True, vmem_limit_bytes=60 * 2**20
        ),
        name="layer",
    )(q, k, v, res, wt, w_in, w_out, ids, gates)


def solution(mesh, ny=8, nz=8, heads=16, dk=64, dv=128):
    def per_device(q, k, v, res, w, w_in, w_out, ids, gates):
        return layer(
            ny, nz, heads, dk, dv, q, k, v, res, w.T, w_in[0], w_out[0], ids.T, gates.T
        )

    tokens = P(("win", "seq"), None)
    experts = P("seq", None, None)
    return jax.shard_map(
        per_device,
        mesh=mesh,
        in_specs=(tokens,) * 4 + (P(None, "seq"), experts, experts, tokens, tokens),
        out_specs=tokens,
        check_vma=False,
    )
```

```python
import functools

import jax
import jax.numpy as jnp
from jax import lax
from jax.experimental import pallas as pl
from jax.experimental.pallas import tpu as pltpu
from jax.sharding import PartitionSpec as P

TOP = 2
CAP = 4
GROUPS = 8
MESH = pl.DeviceIdType.MESH
BF = jnp.bfloat16
F32 = jnp.float32


def dot(a, b, dims=((1,), (0,))):
    return lax.dot_general(a, b, (dims, ((), ())), preferred_element_type=F32)


def layer_kernel(
    ny,
    nz,
    heads,
    dk,
    dv,
    q_hbm,
    k_hbm,
    v_hbm,
    res_hbm,
    wt_hbm,
    win_hbm,
    wout_hbm,
    ids_hbm,
    gates_hbm,
    o_ref,
    q_ref,
    k_ref,
    v_ref,
    res_ref,
    wt_ref,
    ids_ref,
    gates_ref,
    s_loc,
    s_sib,
    s_pair,
    s_pair_out,
    tot,
    p_out,
    r1,
    r2,
    r3,
    prefix,
    w_loc,
    w_all,
    intra,
    attended,
    win,
    wout,
    spread,
    xb,
    xr,
    yb,
    ret,
    s0_send,
    s0_recv,
    s1_send,
    s1_recv,
    s2_send,
    s2_recv,
    s3_send,
    s3_recv,
    s4_send,
    s4_recv,
    w1_send,
    w1_recv,
    met,
    ring_send,
    ring_recv,
    sib_send,
    sib_recv,
    x_send,
    x_recv,
    y_send,
    y_recv,
    win_sem,
):
    n = ny * nz * 2
    row = nz * 2
    length = q_ref.shape[0]
    width = res_ref.shape[1]
    he = wout.shape[0]
    quarter = w_loc.shape[2]
    cut = min(4, ny, nz)
    me = lax.axis_index("seq")
    y, z, c = me // row, lax.rem(me // 2, nz), lax.rem(me, 2)
    at_row = lax.rem(me, row)

    def seq(yy, zz, cc):
        return yy * row + zz * 2 + cc

    def remote(src, dst, ssem, rsem, dev):
        return pltpu.make_async_remote_copy(
            src_ref=src,
            dst_ref=dst,
            send_sem=ssem,
            recv_sem=rsem,
            device_id={"seq": dev},
            device_id_type=MESH,
        )

    def drain(ref, sem):
        pltpu.make_async_copy(ref, ref, sem).wait()

    loads = [
        pltpu.make_async_copy(src, dst, win_sem.at[i])
        for i, (src, dst) in enumerate(
            (
                (k_hbm, k_ref),
                (v_hbm, v_ref),
                (wt_hbm, wt_ref),
                (q_hbm, q_ref),
                (ids_hbm, ids_ref),
                (gates_hbm, gates_ref),
                (res_hbm, res_ref),
                (win_hbm, win),
                (wout_hbm, wout),
            )
        )
    ]
    for load in loads:
        load.start()
    barrier = pltpu.get_barrier_semaphore()

    def greet(dev):
        pl.semaphore_signal(barrier, inc=1, device_id={"seq": dev}, device_id_type=MESH)

    def greet_row(i, _):
        greet(y * row + lax.rem(at_row + i, row))
        return 0

    def greet_column(i, _):
        greet(seq(lax.rem(y + i // 2, ny), z, lax.rem(c + i, 2)))
        return 0

    sib = seq(y, z, 1 - c)
    lax.fori_loop(1, row, greet_row, 0)
    lax.fori_loop(2, 2 * ny, greet_column, 0)

    loads[2].wait()
    for part in range(4):
        w_loc[part] = wt_ref[:, part * quarter : (part + 1) * quarter]
    pl.semaphore_wait(barrier, row + 2 * ny - 3)

    pa, pb = 2 * c, 2 * c + 1

    def keep(part, sem):
        pltpu.make_async_copy(w_loc.at[part], w_all.at[part, y, z, c], sem).start()

    def along_z(i, _):
        to = lax.rem(at_row + i, row)
        part = 2 * lax.rem(to, 2)
        remote(
            w_loc.at[part], w_all.at[part, y, z, c], w1_send.at[0], w1_recv.at[0], y * row + to
        ).start()
        return 0

    def along_y(i, _):
        cc = lax.rem(c + i, 2)
        part = 2 * cc + 1
        remote(
            w_loc.at[part],
            w_all.at[part, y, z, c],
            w1_send.at[1],
            w1_recv.at[1],
            seq(lax.rem(y + i // 2, ny), z, cc),
        ).start()
        return 0

    keep(pa, w1_recv.at[0])
    keep(pb, w1_recv.at[1])
    lax.fori_loop(1, row, along_z, 0)
    lax.fori_loop(1, 2 * ny, along_y, 0)

    loads[0].wait()
    loads[1].wait()

    for p in range(heads // 2):
        kp = k_ref[:, 2 * p * dk : 2 * (p + 1) * dk]
        kv = dot(kp, v_ref[:, 2 * p * dv : 2 * (p + 1) * dv], ((0,), (0,)))
        s_loc[2 * p] = kv[:dk, :dv].astype(BF)
        s_loc[2 * p + 1] = kv[dk:, dv:].astype(BF)

    hh = heads // 2
    own, other = c * hh, (1 - c) * hh
    first_core = c == 0
    remote(s_loc.at[pl.ds(other, hh)], s_sib, s0_send, s0_recv, sib).start()

    def tell(cc, yy):
        pl.semaphore_signal(
            met, inc=1, device_id={"seq": seq(yy, z, cc)}, device_id_type=MESH
        )

    def tell_column(i, _):
        tell(c, lax.rem(y + i, ny))
        return 0

    lax.fori_loop(1, ny, tell_column, 0)

    eye = lax.broadcasted_iota(jnp.int32, (length, length), 0) == lax.broadcasted_iota(
        jnp.int32, (length, length), 1
    )
    below = lax.broadcasted_iota(jnp.int32, (length, length), 1) < lax.broadcasted_iota(
        jnp.int32, (length, length), 0
    )
    above = lax.broadcasted_iota(jnp.int32, (length, length), 0) < lax.broadcasted_iota(
        jnp.int32, (length, length), 1
    )

    for load in loads[4:7]:
        load.wait()

    def column(r):
        return jnp.sum(jnp.where(eye, r, 0.0), axis=1, keepdims=True)

    def turn_of(e):
        dy = ((e >> (row.bit_length() - 1)) + (ny - y)) & (ny - 1)
        dz = ((e >> 1) + (nz - z)) & (nz - 1)
        dc = (e + c) & 1
        return ((dy * row + dz * 2 + dc) * 45) & (n - 1)

    id_row = [turn_of(ids_ref[j : j + 1, :]).astype(F32) for j in range(TOP)]
    id_col = [column(r) for r in id_row]
    gate_col = [column(gates_ref[j : j + 1, :]) for j in range(TOP)]
    place_row, place_col = [], []
    for j in range(TOP):
        row_count, col_count = 0.0, 0.0
        for i in range(TOP):
            row_count = row_count + jnp.where(above & (id_col[i] == id_row[j]), 1.0, 0.0)
            col_count = col_count + jnp.where(below & (id_col[j] == id_row[i]), 1.0, 0.0)
        place_row.append(id_row[j] * CAP + jnp.sum(row_count, axis=0, keepdims=True))
        place_col.append(id_col[j] * CAP + jnp.sum(col_count, axis=1, keepdims=True))
    rows = n * CAP
    r_iota = lax.broadcasted_iota(jnp.int32, (rows, length), 0).astype(F32)
    spread[...] = jnp.where(
        (r_iota == place_row[0]) | (r_iota == place_row[1]), 1.0, 0.0
    ).astype(BF)

    drain(s_sib, s0_recv)
    for i in range(hh):
        both = s_loc[own + i].astype(F32) + s_sib[i].astype(F32)
        s_pair[i] = both.astype(BF)
    pltpu.make_async_copy(s_pair.at[z], r1.at[z], s1_recv).start()

    def far_first(i, size):
        return size // 2 + (1 - 2 * lax.rem(i, 2)) * (i // 2) + size

    def phase1(i, _):
        to = lax.rem(z + far_first(i, nz), nz)
        remote(s_pair.at[to], r1.at[z], s1_send, s1_recv, seq(y, to, c)).start()
        return 0

    lax.fori_loop(1, nz, phase1, 0)

    t_row = lax.broadcasted_iota(jnp.int32, (2 * length, length), 0)
    t_col = lax.broadcasted_iota(jnp.int32, (2 * length, length), 1)
    causal = lax.rem(t_row, length) >= t_col
    first = lax.broadcasted_iota(jnp.int32, (length, 2 * dk), 1) < dk

    def two_heads(p):
        qp = q_ref[:, pl.ds(pl.multiple_of(p * 2 * dk, 2 * dk), 2 * dk)]
        zero = jnp.zeros_like(qp)
        return jnp.concatenate(
            [jnp.where(first, qp, zero), jnp.where(first, zero, qp)], axis=0
        )

    def inside(p, _):
        kp = k_ref[:, pl.ds(pl.multiple_of(p * 2 * dk, 2 * dk), 2 * dk)]
        at = pl.multiple_of(p * 2 * dv, 2 * dv)
        scores = dot(two_heads(p), kp, ((1,), (1,)))
        scores = jnp.where(causal, scores, 0.0).astype(BF)
        vp = v_ref[:, pl.ds(at, 2 * dv)]
        intra[:, pl.ds(at, dv)] = dot(scores[:length], vp[:, :dv])
        intra[:, pl.ds(pl.multiple_of(at + dv, dv), dv)] = dot(scores[length:], vp[:, dv:])
        return 0

    loads[3].wait()
    half = heads // 4
    lax.fori_loop(0, half, inside, 0)

    def mod_y(v):
        return lax.rem(v + 2 * ny, ny)

    def mod_z(v):
        return lax.rem(v + 2 * nz, nz)

    def piece(axis, origin, h, many=1):
        if axis == 0:
            return w_all.at[pa, origin, pl.ds(h * (nz // cut), many * (nz // cut))]
        return w_all.at[pb, pl.ds(h * (ny // cut), many * (ny // cut)), origin]

    def pieces(axis, way, step):
        size = ny if axis == 0 else nz
        mine = tuple(range(way * cut // 2, (way + 1) * cut // 2))
        if 2 * step > size:
            return ()
        return mine if 2 * step == size else mine + tuple(set(range(cut)) - set(mine))

    def to_sibling(ref):
        remote(ref, ref, sib_send, sib_recv, sib).start()

    def ring_copy(axis, way, step, h):
        mod, at = (mod_y, y) if axis == 0 else (mod_z, z)
        sign = 1 if way == 0 else -1
        ref = piece(axis, mod(at - sign * (step - 1)), h)
        dev = seq(mod(at + sign), z, c) if axis == 0 else seq(y, mod(at + sign), c)
        place = (axis, way, step - 1, h)
        return remote(ref, ref, ring_send.at[place], ring_recv.at[place], dev)

    def ring_step(step):
        for turn in range(cut):
            for axis in (0, 1):
                mod, at = (mod_y, y) if axis == 0 else (mod_z, z)
                for way in (0, 1):
                    order = pieces(axis, way, step)
                    if turn < len(order):
                        h = order[turn]
                        origin = mod(at - step if way == 0 else at + step)
                        drain(piece(axis, origin, h), ring_recv.at[axis, way, step - 1, h])
                        if h in pieces(axis, way, step + 1):
                            ring_copy(axis, way, step + 1, h).start()
                        if turn == len(order) - 1:
                            to_sibling(piece(axis, origin, min(order), len(order)))

    def ring_open(axis):
        for turn in range(cut):
            for way in (0, 1):
                if turn < len(pieces(axis, way, 1)):
                    ring_copy(axis, way, 1, pieces(axis, way, 1)[turn]).start()

    drain(w_all.at[pa, y], w1_recv.at[0])
    ring_open(0)
    drain(w_all.at[pb, :, z], w1_recv.at[1])
    ring_open(1)
    to_sibling(w_all.at[pa, y])
    to_sibling(w_all.at[pb, :, z])

    lax.fori_loop(half, heads // 2, inside, 0)

    drain(r1, s1_recv)
    total = r1[0].astype(F32)
    for i in range(1, nz):
        total = total + r1[i].astype(F32)
    tot[...] = total.astype(BF)
    pltpu.make_async_copy(tot, r2.at[y], s2_recv).start()

    def phase2(i, _):
        yy = lax.rem(y + far_first(i, ny), ny)
        remote(tot, r2.at[y], s2_send, s2_recv, seq(yy, z, c)).start()
        return 0

    lax.fori_loop(1, ny, phase2, 0)

    ring_step(1)

    drain(r2, s2_recv)
    run = jnp.zeros(total.shape, F32)
    for yy in range(ny):
        run = run + jnp.where(yy < y, r2[yy].astype(F32), 0.0)
    for i in range(nz):
        p_out[i] = run.astype(BF)
        if i < nz - 1:
            run = run + r1[i].astype(F32)
    pltpu.make_async_copy(p_out.at[z], r3.at[z], s3_recv).start()

    def phase3(i, _):
        to = lax.rem(z + far_first(i, nz), nz)
        remote(p_out.at[to], r3.at[z], s3_send, s3_recv, seq(y, to, c)).start()
        return 0

    lax.fori_loop(1, nz, phase3, 0)

    ring_step(2)

    drain(r3, s3_recv)
    for i in range(hh):
        chip = r3[i].astype(F32)
        theirs = chip + jnp.where(first_core, s_loc[own + i].astype(F32), 0.0)
        s_pair_out[i] = theirs.astype(BF)
    remote(s_pair_out, prefix.at[pl.ds(own, hh)], s4_send, s4_recv, sib).start()
    for i in range(hh):
        chip = r3[i].astype(F32)
        mine = chip + jnp.where(first_core, 0.0, s_sib[i].astype(F32))
        prefix[own + i] = mine.astype(BF)

    ring_step(3)

    position = me * length + lax.broadcasted_iota(jnp.int32, (length, 1), 0)
    scaling = lax.rsqrt((position.astype(F32) + 1.0) * dk)

    def before(p):
        past = prefix[pl.ds(2 * p, 2)].reshape(2 * dk, dv)
        earlier = dot(two_heads(p), past)
        for h in range(2):
            cols = pl.ds(pl.multiple_of((2 * p + h) * dv, dv), dv)
            attended[:, cols] = (
                (intra[:, cols] + earlier[h * length : (h + 1) * length]) * scaling
            ).astype(BF)

    for p in range(hh // 2):
        before(own // 2 + p)
    drain(prefix.at[pl.ds(other, hh)], s4_recv)
    for p in range(hh // 2):
        before(other // 2 + p)

    for step in range(4, max(ny, nz) // 2 + 1):
        ring_step(step)

    def project(part):
        cols = pl.ds(pl.multiple_of(part * quarter, quarter), quarter)
        return dot(attended[:, cols], w_all[part].reshape(width, quarter), ((1,), (1,)))

    projected = project(pa) + project(pb)
    drain(w_all.at[pl.ds(2 * (1 - c), 2)], sib_recv)
    projected = projected + (project(2 * (1 - c)) + project(2 * (1 - c) + 1))
    hidden = (res_ref[...].astype(F32) + projected).astype(BF)
    hidden_float = hidden.astype(F32)
    intra[:, :width] = hidden_float
    normed = (
        hidden_float
        * lax.rsqrt(jnp.mean(hidden_float * hidden_float, axis=-1, keepdims=True) + 1e-06)
    ).astype(BF)

    def offset(i):
        j = lax.rem(i * 37, n)
        return j // row, lax.rem(j // 2, nz), lax.rem(j, 2)

    def ahead(i):
        dy, dz, dc = offset(i)
        return seq(lax.rem(y + dy, ny), lax.rem(z + dz, nz), lax.rem(c + dc, 2))

    def behind(i):
        dy, dz, dc = offset(i)
        return seq(lax.rem(y - dy + ny, ny), lax.rem(z - dz + nz, nz), lax.rem(c - dc + 2, 2))

    per = n // GROUPS
    pl.semaphore_wait(met, ny - 1)

    def fill(g):
        mine = spread[pl.ds(pl.multiple_of(g * per * CAP, per * CAP), per * CAP)]
        xb[pl.ds(g * per, per)] = dot(mine, normed).astype(BF).reshape(per, CAP, width)

    def dispatch(i, _):
        remote(xb.at[i], xr.at[i], x_send, x_recv.at[i // per], ahead(i)).start()
        return 0

    fill(0)
    pltpu.make_async_copy(xb.at[0], xr.at[0], x_recv.at[0]).start()
    lax.fori_loop(1, per, dispatch, 0)
    for g in range(1, GROUPS):
        fill(g)
        lax.fori_loop(g * per, (g + 1) * per, dispatch, 0)

    loads[7].wait()
    loads[8].wait()

    def expert(g):
        lo = g * per
        drain(xr.at[pl.ds(lo, per)], x_recv.at[g])
        x = xr[pl.ds(lo, per)].reshape(per * CAP, width)
        act = dot(x, win[...])
        gate, up = act[:, :he], act[:, he:]
        inner = (gate / (1.0 + jnp.exp(-gate)) * up).astype(BF)
        yb[pl.ds(lo, per)] = dot(inner, wout[...]).astype(BF).reshape(per, CAP, width)

    def give_back(i, _):
        to = behind(i)
        remote(yb.at[i], ret.at[i], y_send, y_recv.at[i // per], to).start()
        return 0

    expert(0)
    pltpu.make_async_copy(yb.at[0], ret.at[0], y_recv.at[0]).start()
    lax.fori_loop(1, per, give_back, 0)

    def group(g, _):
        expert(g)
        lax.fori_loop(g * per, (g + 1) * per, give_back, 0)
        return 0

    lax.fori_loop(1, GROUPS, group, 0)

    wide = per * CAP
    r_lane = lax.broadcasted_iota(jnp.int32, (length, wide), 1).astype(F32)
    combined = jnp.zeros((length, width), F32)
    for g in range(GROUPS):
        picks = jnp.concatenate(
            [
                jnp.where(r_lane + g * wide == place_col[j], 1.0, 0.0).astype(BF)
                for j in range(TOP)
            ],
            axis=0,
        )
        drain(ret.at[pl.ds(g * per, per)], y_recv.at[g])
        picked = dot(picks, ret[g * per : (g + 1) * per].reshape(wide, width))
        combined = combined + (picked[:length] * gate_col[0] + picked[length:] * gate_col[1])
    o_ref[...] = (intra[:, :width] + combined).astype(BF)

    drain(s_sib, s0_send)
    drain(r1.at[pl.ds(0, nz - 1)], s1_send)
    drain(r2.at[pl.ds(0, ny - 1)], s2_send)
    drain(r3.at[pl.ds(0, nz - 1)], s3_send)
    drain(s_sib, s4_send)
    drain(w_all.at[0, 0, pl.ds(0, nz - 1)], w1_send.at[0])
    drain(w_loc.at[0], w1_send.at[0])
    drain(w_all.at[0, pl.ds(0, ny - 1), 0], w1_send.at[1])
    drain(w_loc.at[0], w1_send.at[1])
    for axis in (0, 1):
        for step in range(1, max(ny, nz) // 2 + 1):
            for way in (0, 1):
                for h in pieces(axis, way, step):
                    ring_copy(axis, way, step, h).wait_send()
    drain(w_all.at[pl.ds(2 * c, 2)], sib_send)
    drain(xb.at[pl.ds(0, n - 1)], x_send)
    drain(yb.at[pl.ds(0, n - 1)], y_send)


def layer(ny, nz, heads, dk, dv, q, k, v, res, wt, w_in, w_out, ids, gates):
    n = ny * nz * 2
    length, width = res.shape
    cols = wt.shape[0]
    quarter = heads * dv // 4
    vmem = pl.BlockSpec(memory_space=pltpu.VMEM)
    hbm = pl.BlockSpec(memory_space=pl.ANY)
    steps = max(ny, nz) // 2
    dma = pltpu.SemaphoreType.DMA
    rows = (n, CAP, width)
    return pl.pallas_call(
        functools.partial(layer_kernel, ny, nz, heads, dk, dv),
        out_shape=pltpu.VMEM((length, width), BF),
        in_specs=[hbm] * 9,
        out_specs=vmem,
        scratch_shapes=[
            *[pltpu.VMEM(a.shape, a.dtype) for a in (q, k, v, res, wt, ids, gates)],
            pltpu.VMEM((heads, dk, dv), BF),
            pltpu.VMEM((nz, dk, dv), BF),
            pltpu.VMEM((nz, dk, dv), BF),
            pltpu.VMEM((nz, dk, dv), BF),
            pltpu.VMEM((dk, dv), BF),
            pltpu.VMEM((nz, dk, dv), BF),
            pltpu.VMEM((nz, dk, dv), BF),
            pltpu.VMEM((ny, dk, dv), BF),
            pltpu.VMEM((nz, dk, dv), BF),
            pltpu.VMEM((heads, dk, dv), BF),
            pltpu.VMEM((4, cols, quarter), BF),
            pltpu.VMEM((4, ny, nz, 2, cols, quarter), BF),
            pltpu.VMEM((length, heads * dv), F32),
            pltpu.VMEM((length, heads * dv), BF),
            pltpu.VMEM(w_in.shape, BF),
            pltpu.VMEM(w_out.shape, BF),
            pltpu.VMEM((n * CAP, length), BF),
            pltpu.VMEM(rows, BF),
            pltpu.VMEM(rows, BF),
            pltpu.VMEM(rows, BF),
            pltpu.VMEM(rows, BF),
            *[dma] * 10,
            dma((2,)),
            dma((2,)),
            pltpu.SemaphoreType.REGULAR,
            dma((2, 2, steps, 4)),
            dma((2, 2, steps, 4)),
            dma,
            dma,
            dma,
            dma((GROUPS,)),
            dma,
            dma((GROUPS,)),
            dma((9,)),
        ],
        compiler_params=pltpu.CompilerParams(
            collective_id=0, has_side_effects=True, vmem_limit_bytes=60 * 2**20
        ),
        name="layer",
    )(q, k, v, res, wt, w_in, w_out, ids, gates)


def solution(mesh, ny=8, nz=8, heads=16, dk=64, dv=128):
    def per_device(q, k, v, res, w, w_in, w_out, ids, gates):
        return layer(
            ny, nz, heads, dk, dv, q, k, v, res, w.T, w_in[0], w_out[0], ids.T, gates.T
        )

    tokens = P(("win", "seq"), None)
    experts = P("seq", None, None)
    return jax.shard_map(
        per_device,
        mesh=mesh,
        in_specs=(tokens,) * 4 + (P(None, "seq"), experts, experts, tokens, tokens),
        out_specs=tokens,
        check_vma=False,
    )
```

```python
import functools

import jax
import jax.numpy as jnp
from jax import lax
from jax.experimental import pallas as pl
from jax.experimental.pallas import tpu as pltpu
from jax.sharding import PartitionSpec as P

TOP = 2
CAP = 4
GROUPS = 4
MESH = pl.DeviceIdType.MESH
BF = jnp.bfloat16
F32 = jnp.float32


def dot(a, b, dims=((1,), (0,))):
    return lax.dot_general(a, b, (dims, ((), ())), preferred_element_type=F32)


def layer_kernel(
    ny,
    nz,
    heads,
    dk,
    dv,
    q_hbm,
    k_hbm,
    v_hbm,
    res_hbm,
    wt_hbm,
    win_hbm,
    wout_hbm,
    ids_hbm,
    gates_hbm,
    o_ref,
    q_ref,
    k_ref,
    v_ref,
    res_ref,
    wt_ref,
    ids_ref,
    gates_ref,
    s_loc,
    s_sib,
    s_pair,
    s_pair_out,
    tot,
    p_out,
    r1,
    r2,
    r3,
    prefix,
    w_loc,
    w_all,
    intra,
    attended,
    win,
    wout,
    spread,
    xb,
    xr,
    yb,
    ret,
    s0_send,
    s0_recv,
    s1_send,
    s1_recv,
    s2_send,
    s2_recv,
    s3_send,
    s3_recv,
    s4_send,
    s4_recv,
    w1_send,
    w1_recv,
    met,
    ring_send,
    ring_recv,
    sib_send,
    sib_recv,
    x_send,
    x_recv,
    y_send,
    y_recv,
    win_sem,
):
    n = ny * nz * 2
    row = nz * 2
    length = q_ref.shape[0]
    width = res_ref.shape[1]
    he = wout.shape[0]
    quarter = w_loc.shape[2]
    cut = min(4, ny, nz)
    me = lax.axis_index("seq")
    y, z, c = me // row, lax.rem(me // 2, nz), lax.rem(me, 2)
    at_row = lax.rem(me, row)

    def seq(yy, zz, cc):
        return yy * row + zz * 2 + cc

    def remote(src, dst, ssem, rsem, dev):
        return pltpu.make_async_remote_copy(
            src_ref=src,
            dst_ref=dst,
            send_sem=ssem,
            recv_sem=rsem,
            device_id={"seq": dev},
            device_id_type=MESH,
        )

    def drain(ref, sem):
        pltpu.make_async_copy(ref, ref, sem).wait()

    loads = [
        pltpu.make_async_copy(src, dst, win_sem.at[i])
        for i, (src, dst) in enumerate(
            (
                (k_hbm, k_ref),
                (v_hbm, v_ref),
                (wt_hbm, wt_ref),
                (q_hbm, q_ref),
                (ids_hbm, ids_ref),
                (gates_hbm, gates_ref),
                (res_hbm, res_ref),
                (win_hbm, win),
                (wout_hbm, wout),
            )
        )
    ]
    for load in loads:
        load.start()
    barrier = pltpu.get_barrier_semaphore()

    def far_first(i, size):
        return size // 2 + (1 - 2 * lax.rem(i, 2)) * (i // 2) + size

    def greet(dev):
        pl.semaphore_signal(barrier, inc=1, device_id={"seq": dev}, device_id_type=MESH)

    def greet_row(i, _):
        greet(y * row + lax.rem(at_row + far_first(i, row), row))
        return 0

    def greet_column(i, _):
        greet(seq(lax.rem(y + far_first(i // 2, ny), ny), z, lax.rem(c + i, 2)))
        return 0

    sib = seq(y, z, 1 - c)
    lax.fori_loop(1, row, greet_row, 0)
    lax.fori_loop(2, 2 * ny, greet_column, 0)

    loads[2].wait()
    for part in range(4):
        w_loc[part] = wt_ref[:, part * quarter : (part + 1) * quarter]
    pl.semaphore_wait(barrier, row + 2 * ny - 3)

    pa, pb = 2 * c, 2 * c + 1

    def keep(part, sem):
        pltpu.make_async_copy(w_loc.at[part], w_all.at[part, y, z, c], sem).start()

    def along_z(i, _):
        to = lax.rem(at_row + far_first(i, row), row)
        part = 2 * lax.rem(to, 2)
        remote(
            w_loc.at[part], w_all.at[part, y, z, c], w1_send.at[0], w1_recv.at[0], y * row + to
        ).start()
        return 0

    def to_column(yy, cc):
        part = 2 * cc + 1
        remote(
            w_loc.at[part],
            w_all.at[part, y, z, c],
            w1_send.at[1],
            w1_recv.at[1],
            seq(yy, z, cc),
        ).start()

    def along_y(i, _):
        to_column(lax.rem(y + far_first(i // 2, ny), ny), lax.rem(c + i, 2))
        return 0

    keep(pa, w1_recv.at[0])
    keep(pb, w1_recv.at[1])
    lax.fori_loop(1, row, along_z, 0)
    lax.fori_loop(2, 2 * ny, along_y, 0)
    to_column(y, 1 - c)

    loads[0].wait()
    loads[1].wait()

    for p in range(heads // 2):
        kp = k_ref[:, 2 * p * dk : 2 * (p + 1) * dk]
        kv = dot(kp, v_ref[:, 2 * p * dv : 2 * (p + 1) * dv], ((0,), (0,)))
        s_loc[2 * p] = kv[:dk, :dv].astype(BF)
        s_loc[2 * p + 1] = kv[dk:, dv:].astype(BF)

    hh = heads // 2
    own, other = c * hh, (1 - c) * hh
    first_core = c == 0
    remote(s_loc.at[pl.ds(other, hh)], s_sib, s0_send, s0_recv, sib).start()

    def tell(cc, yy):
        pl.semaphore_signal(
            met, inc=1, device_id={"seq": seq(yy, z, cc)}, device_id_type=MESH
        )

    def tell_column(i, _):
        tell(c, lax.rem(y + i, ny))
        return 0

    lax.fori_loop(1, ny, tell_column, 0)

    eye = lax.broadcasted_iota(jnp.int32, (length, length), 0) == lax.broadcasted_iota(
        jnp.int32, (length, length), 1
    )
    below = lax.broadcasted_iota(jnp.int32, (length, length), 1) < lax.broadcasted_iota(
        jnp.int32, (length, length), 0
    )
    above = lax.broadcasted_iota(jnp.int32, (length, length), 0) < lax.broadcasted_iota(
        jnp.int32, (length, length), 1
    )

    for load in loads[4:7]:
        load.wait()

    def column(r):
        return jnp.sum(jnp.where(eye, r, 0.0), axis=1, keepdims=True)

    def turn_of(e):
        dy = ((e >> (row.bit_length() - 1)) + (ny - y)) & (ny - 1)
        dz = ((e >> 1) + (nz - z)) & (nz - 1)
        dc = (e + c) & 1
        return ((dy * row + dz * 2 + dc) * 45) & (n - 1)

    id_row = [turn_of(ids_ref[j : j + 1, :]).astype(F32) for j in range(TOP)]
    id_col = [column(r) for r in id_row]
    gate_col = [column(gates_ref[j : j + 1, :]) for j in range(TOP)]
    place_row, place_col = [], []
    for j in range(TOP):
        row_count, col_count = 0.0, 0.0
        for i in range(TOP):
            row_count = row_count + jnp.where(above & (id_col[i] == id_row[j]), 1.0, 0.0)
            col_count = col_count + jnp.where(below & (id_col[j] == id_row[i]), 1.0, 0.0)
        place_row.append(id_row[j] * CAP + jnp.sum(row_count, axis=0, keepdims=True))
        place_col.append(id_col[j] * CAP + jnp.sum(col_count, axis=1, keepdims=True))
    rows = n * CAP
    r_iota = lax.broadcasted_iota(jnp.int32, (rows, length), 0).astype(F32)
    spread[...] = jnp.where(
        (r_iota == place_row[0]) | (r_iota == place_row[1]), 1.0, 0.0
    ).astype(BF)

    drain(s_sib, s0_recv)
    for i in range(hh):
        both = s_loc[own + i].astype(F32) + s_sib[i].astype(F32)
        s_pair[i] = both.astype(BF)
    pltpu.make_async_copy(s_pair.at[z], r1.at[z], s1_recv).start()

    def phase1(i, _):
        to = lax.rem(z + far_first(i, nz), nz)
        remote(s_pair.at[to], r1.at[z], s1_send, s1_recv, seq(y, to, c)).start()
        return 0

    lax.fori_loop(1, nz, phase1, 0)

    t_row = lax.broadcasted_iota(jnp.int32, (2 * length, length), 0)
    t_col = lax.broadcasted_iota(jnp.int32, (2 * length, length), 1)
    causal = lax.rem(t_row, length) >= t_col
    first = lax.broadcasted_iota(jnp.int32, (length, 2 * dk), 1) < dk

    def two_heads(p):
        qp = q_ref[:, pl.ds(pl.multiple_of(p * 2 * dk, 2 * dk), 2 * dk)]
        zero = jnp.zeros_like(qp)
        return jnp.concatenate(
            [jnp.where(first, qp, zero), jnp.where(first, zero, qp)], axis=0
        )

    def inside(p, _):
        kp = k_ref[:, pl.ds(pl.multiple_of(p * 2 * dk, 2 * dk), 2 * dk)]
        at = pl.multiple_of(p * 2 * dv, 2 * dv)
        scores = dot(two_heads(p), kp, ((1,), (1,)))
        scores = jnp.where(causal, scores, 0.0).astype(BF)
        vp = v_ref[:, pl.ds(at, 2 * dv)]
        intra[:, pl.ds(at, dv)] = dot(scores[:length], vp[:, :dv])
        intra[:, pl.ds(pl.multiple_of(at + dv, dv), dv)] = dot(scores[length:], vp[:, dv:])
        return 0

    loads[3].wait()
    half = heads // 4
    lax.fori_loop(0, half, inside, 0)

    def mod_y(v):
        return lax.rem(v + 2 * ny, ny)

    def mod_z(v):
        return lax.rem(v + 2 * nz, nz)

    def piece(axis, origin, h, many=1):
        if axis == 0:
            return w_all.at[pa, origin, pl.ds(h * (nz // cut), many * (nz // cut))]
        return w_all.at[pb, pl.ds(h * (ny // cut), many * (ny // cut)), origin]

    def pieces(axis, way, step):
        size = ny if axis == 0 else nz
        mine = tuple(range(way * cut // 2, (way + 1) * cut // 2))
        if 2 * step > size:
            return ()
        return mine if 2 * step == size else mine + tuple(set(range(cut)) - set(mine))

    def to_sibling(ref):
        remote(ref, ref, sib_send, sib_recv, sib).start()

    def ring_copy(axis, way, step, h):
        mod, at = (mod_y, y) if axis == 0 else (mod_z, z)
        sign = 1 if way == 0 else -1
        ref = piece(axis, mod(at - sign * (step - 1)), h)
        dev = seq(mod(at + sign), z, c) if axis == 0 else seq(y, mod(at + sign), c)
        place = (axis, way, step - 1, h)
        return remote(ref, ref, ring_send.at[place], ring_recv.at[place], dev)

    def ring_step(step):
        for turn in range(cut):
            for axis in (0, 1):
                mod, at = (mod_y, y) if axis == 0 else (mod_z, z)
                for way in (0, 1):
                    order = pieces(axis, way, step)
                    if turn < len(order):
                        h = order[turn]
                        origin = mod(at - step if way == 0 else at + step)
                        drain(piece(axis, origin, h), ring_recv.at[axis, way, step - 1, h])
                        if h in pieces(axis, way, step + 1):
                            ring_copy(axis, way, step + 1, h).start()
                        if turn == len(order) - 1:
                            to_sibling(piece(axis, origin, min(order), len(order)))

    def ring_open(axis):
        for turn in range(cut):
            for way in (0, 1):
                if turn < len(pieces(axis, way, 1)):
                    ring_copy(axis, way, 1, pieces(axis, way, 1)[turn]).start()

    drain(w_all.at[pa, y], w1_recv.at[0])
    ring_open(0)
    drain(w_all.at[pb, :, z], w1_recv.at[1])
    ring_open(1)
    to_sibling(w_all.at[pa, y])
    to_sibling(w_all.at[pb, :, z])

    lax.fori_loop(half, heads // 2, inside, 0)

    drain(r1, s1_recv)
    total = r1[0].astype(F32)
    for i in range(1, nz):
        total = total + r1[i].astype(F32)
    tot[...] = total.astype(BF)
    pltpu.make_async_copy(tot, r2.at[y], s2_recv).start()

    def phase2(i, _):
        yy = lax.rem(y + far_first(i, ny), ny)
        remote(tot, r2.at[y], s2_send, s2_recv, seq(yy, z, c)).start()
        return 0

    lax.fori_loop(1, ny, phase2, 0)

    ring_step(1)

    drain(r2, s2_recv)
    run = jnp.zeros(total.shape, F32)
    for yy in range(ny):
        run = run + jnp.where(yy < y, r2[yy].astype(F32), 0.0)
    for i in range(nz):
        p_out[i] = run.astype(BF)
        if i < nz - 1:
            run = run + r1[i].astype(F32)
    pltpu.make_async_copy(p_out.at[z], r3.at[z], s3_recv).start()

    def phase3(i, _):
        to = lax.rem(z + far_first(i, nz), nz)
        remote(p_out.at[to], r3.at[z], s3_send, s3_recv, seq(y, to, c)).start()
        return 0

    lax.fori_loop(1, nz, phase3, 0)

    ring_step(2)

    drain(r3, s3_recv)
    for i in range(hh):
        chip = r3[i].astype(F32)
        theirs = chip + jnp.where(first_core, s_loc[own + i].astype(F32), 0.0)
        s_pair_out[i] = theirs.astype(BF)
    remote(s_pair_out, prefix.at[pl.ds(own, hh)], s4_send, s4_recv, sib).start()
    for i in range(hh):
        chip = r3[i].astype(F32)
        mine = chip + jnp.where(first_core, 0.0, s_sib[i].astype(F32))
        prefix[own + i] = mine.astype(BF)

    ring_step(3)

    position = me * length + lax.broadcasted_iota(jnp.int32, (length, 1), 0)
    scaling = lax.rsqrt((position.astype(F32) + 1.0) * dk)

    def before(p):
        past = prefix[pl.ds(2 * p, 2)].reshape(2 * dk, dv)
        earlier = dot(two_heads(p), past)
        for h in range(2):
            cols = pl.ds(pl.multiple_of((2 * p + h) * dv, dv), dv)
            attended[:, cols] = (
                (intra[:, cols] + earlier[h * length : (h + 1) * length]) * scaling
            ).astype(BF)

    for p in range(hh // 2):
        before(own // 2 + p)
    drain(prefix.at[pl.ds(other, hh)], s4_recv)
    for p in range(hh // 2):
        before(other // 2 + p)

    for step in range(4, max(ny, nz) // 2 + 1):
        ring_step(step)

    def project(part):
        cols = pl.ds(pl.multiple_of(part * quarter, quarter), quarter)
        return dot(attended[:, cols], w_all[part].reshape(width, quarter), ((1,), (1,)))

    projected = project(pa) + project(pb)
    drain(w_all.at[pl.ds(2 * (1 - c), 2)], sib_recv)
    projected = projected + (project(2 * (1 - c)) + project(2 * (1 - c) + 1))
    hidden = (res_ref[...].astype(F32) + projected).astype(BF)
    hidden_float = hidden.astype(F32)
    intra[:, :width] = hidden_float
    normed = (
        hidden_float
        * lax.rsqrt(jnp.mean(hidden_float * hidden_float, axis=-1, keepdims=True) + 1e-06)
    ).astype(BF)

    def offset(i):
        j = lax.rem(i * 37, n)
        return j // row, lax.rem(j // 2, nz), lax.rem(j, 2)

    def ahead(i):
        dy, dz, dc = offset(i)
        return seq(lax.rem(y + dy, ny), lax.rem(z + dz, nz), lax.rem(c + dc, 2))

    def behind(i):
        dy, dz, dc = offset(i)
        return seq(lax.rem(y - dy + ny, ny), lax.rem(z - dz + nz, nz), lax.rem(c - dc + 2, 2))

    per = n // GROUPS
    pl.semaphore_wait(met, ny - 1)

    def fill(g):
        mine = spread[pl.ds(pl.multiple_of(g * per * CAP, per * CAP), per * CAP)]
        xb[pl.ds(g * per, per)] = dot(mine, normed).astype(BF).reshape(per, CAP, width)

    def dispatch(i, _):
        remote(xb.at[i], xr.at[i], x_send, x_recv.at[i // per], ahead(i)).start()
        return 0

    fill(0)
    pltpu.make_async_copy(xb.at[0], xr.at[0], x_recv.at[0]).start()
    lax.fori_loop(1, per, dispatch, 0)
    for g in range(1, GROUPS):
        fill(g)
        lax.fori_loop(g * per, (g + 1) * per, dispatch, 0)

    loads[7].wait()
    loads[8].wait()

    def expert(g):
        lo = g * per
        drain(xr.at[pl.ds(lo, per)], x_recv.at[g])
        x = xr[pl.ds(lo, per)].reshape(per * CAP, width)
        act = dot(x, win[...])
        gate, up = act[:, :he], act[:, he:]
        inner = (gate / (1.0 + jnp.exp(-gate)) * up).astype(BF)
        yb[pl.ds(lo, per)] = dot(inner, wout[...]).astype(BF).reshape(per, CAP, width)

    def give_back(i, _):
        to = behind(i)
        remote(yb.at[i], ret.at[i], y_send, y_recv.at[i // per], to).start()
        return 0

    expert(0)
    pltpu.make_async_copy(yb.at[0], ret.at[0], y_recv.at[0]).start()
    lax.fori_loop(1, per, give_back, 0)

    def group(g, _):
        expert(g)
        lax.fori_loop(g * per, (g + 1) * per, give_back, 0)
        return 0

    lax.fori_loop(1, GROUPS, group, 0)

    wide = per * CAP
    r_lane = lax.broadcasted_iota(jnp.int32, (length, wide), 1).astype(F32)
    combined = jnp.zeros((length, width), F32)
    for g in range(GROUPS):
        picks = jnp.concatenate(
            [
                jnp.where(r_lane + g * wide == place_col[j], 1.0, 0.0).astype(BF)
                for j in range(TOP)
            ],
            axis=0,
        )
        drain(ret.at[pl.ds(g * per, per)], y_recv.at[g])
        picked = dot(picks, ret[g * per : (g + 1) * per].reshape(wide, width))
        combined = combined + (picked[:length] * gate_col[0] + picked[length:] * gate_col[1])
    o_ref[...] = (intra[:, :width] + combined).astype(BF)

    drain(s_sib, s0_send)
    drain(r1.at[pl.ds(0, nz - 1)], s1_send)
    drain(r2.at[pl.ds(0, ny - 1)], s2_send)
    drain(r3.at[pl.ds(0, nz - 1)], s3_send)
    drain(s_sib, s4_send)
    drain(w_all.at[0, 0, pl.ds(0, nz - 1)], w1_send.at[0])
    drain(w_loc.at[0], w1_send.at[0])
    drain(w_all.at[0, pl.ds(0, ny - 1), 0], w1_send.at[1])
    drain(w_loc.at[0], w1_send.at[1])
    for axis in (0, 1):
        for step in range(1, max(ny, nz) // 2 + 1):
            for way in (0, 1):
                for h in pieces(axis, way, step):
                    ring_copy(axis, way, step, h).wait_send()
    drain(w_all.at[pl.ds(2 * c, 2)], sib_send)
    drain(xb.at[pl.ds(0, n - 1)], x_send)
    drain(yb.at[pl.ds(0, n - 1)], y_send)


def layer(ny, nz, heads, dk, dv, q, k, v, res, wt, w_in, w_out, ids, gates):
    n = ny * nz * 2
    length, width = res.shape
    cols = wt.shape[0]
    quarter = heads * dv // 4
    vmem = pl.BlockSpec(memory_space=pltpu.VMEM)
    hbm = pl.BlockSpec(memory_space=pl.ANY)
    steps = max(ny, nz) // 2
    dma = pltpu.SemaphoreType.DMA
    rows = (n, CAP, width)
    return pl.pallas_call(
        functools.partial(layer_kernel, ny, nz, heads, dk, dv),
        out_shape=pltpu.VMEM((length, width), BF),
        in_specs=[hbm] * 9,
        out_specs=vmem,
        scratch_shapes=[
            *[pltpu.VMEM(a.shape, a.dtype) for a in (q, k, v, res, wt, ids, gates)],
            pltpu.VMEM((heads, dk, dv), BF),
            pltpu.VMEM((nz, dk, dv), BF),
            pltpu.VMEM((nz, dk, dv), BF),
            pltpu.VMEM((nz, dk, dv), BF),
            pltpu.VMEM((dk, dv), BF),
            pltpu.VMEM((nz, dk, dv), BF),
            pltpu.VMEM((nz, dk, dv), BF),
            pltpu.VMEM((ny, dk, dv), BF),
            pltpu.VMEM((nz, dk, dv), BF),
            pltpu.VMEM((heads, dk, dv), BF),
            pltpu.VMEM((4, cols, quarter), BF),
            pltpu.VMEM((4, ny, nz, 2, cols, quarter), BF),
            pltpu.VMEM((length, heads * dv), F32),
            pltpu.VMEM((length, heads * dv), BF),
            pltpu.VMEM(w_in.shape, BF),
            pltpu.VMEM(w_out.shape, BF),
            pltpu.VMEM((n * CAP, length), BF),
            pltpu.VMEM(rows, BF),
            pltpu.VMEM(rows, BF),
            pltpu.VMEM(rows, BF),
            pltpu.VMEM(rows, BF),
            *[dma] * 10,
            dma((2,)),
            dma((2,)),
            pltpu.SemaphoreType.REGULAR,
            dma((2, 2, steps, 4)),
            dma((2, 2, steps, 4)),
            dma,
            dma,
            dma,
            dma((GROUPS,)),
            dma,
            dma((GROUPS,)),
            dma((9,)),
        ],
        compiler_params=pltpu.CompilerParams(
            collective_id=0, has_side_effects=True, vmem_limit_bytes=60 * 2**20
        ),
        name="layer",
    )(q, k, v, res, wt, w_in, w_out, ids, gates)


def solution(mesh, ny=8, nz=8, heads=16, dk=64, dv=128):
    def per_device(q, k, v, res, w, w_in, w_out, ids, gates):
        return layer(
            ny, nz, heads, dk, dv, q, k, v, res, w.T, w_in[0], w_out[0], ids.T, gates.T
        )

    tokens = P(("win", "seq"), None)
    experts = P("seq", None, None)
    return jax.shard_map(
        per_device,
        mesh=mesh,
        in_specs=(tokens,) * 4 + (P(None, "seq"), experts, experts, tokens, tokens),
        out_specs=tokens,
        check_vma=False,
    )
```

```python
import functools

import jax
import jax.numpy as jnp
from jax import lax
from jax.experimental import pallas as pl
from jax.experimental.pallas import tpu as pltpu
from jax.sharding import PartitionSpec as P

TOP = 2
CAP = 4
GROUPS = 4
MESH = pl.DeviceIdType.MESH
BF = jnp.bfloat16
F32 = jnp.float32


def dot(a, b, dims=((1,), (0,))):
    return lax.dot_general(a, b, (dims, ((), ())), preferred_element_type=F32)


def layer_kernel(
    ny,
    nz,
    heads,
    dk,
    dv,
    q_hbm,
    k_hbm,
    v_hbm,
    res_hbm,
    wt_hbm,
    win_hbm,
    wout_hbm,
    ids_hbm,
    gates_hbm,
    o_ref,
    q_ref,
    k_ref,
    v_ref,
    res_ref,
    wt_ref,
    ids_ref,
    gates_ref,
    s_loc,
    s_sib,
    s_pair,
    s_pair_out,
    tot,
    p_out,
    r1,
    r2,
    r3,
    prefix,
    w_loc,
    w_all,
    intra,
    attended,
    win,
    wout,
    spread,
    xb,
    xr,
    yb,
    ret,
    s0_send,
    s0_recv,
    s1_send,
    s1_recv,
    s2_send,
    s2_recv,
    s3_send,
    s3_recv,
    s4_send,
    s4_recv,
    w1_send,
    w1_recv,
    met,
    ring_send,
    ring_recv,
    sib_send,
    sib_recv,
    x_send,
    x_recv,
    y_send,
    y_recv,
    win_sem,
):
    n = ny * nz * 2
    row = nz * 2
    length = q_ref.shape[0]
    width = res_ref.shape[1]
    he = wout.shape[0]
    quarter = w_loc.shape[2]
    cut = min(4, ny, nz)
    me = lax.axis_index("seq")
    y, z, c = me // row, lax.rem(me // 2, nz), lax.rem(me, 2)
    at_row = lax.rem(me, row)

    def seq(yy, zz, cc):
        return yy * row + zz * 2 + cc

    def remote(src, dst, ssem, rsem, dev):
        return pltpu.make_async_remote_copy(
            src_ref=src,
            dst_ref=dst,
            send_sem=ssem,
            recv_sem=rsem,
            device_id={"seq": dev},
            device_id_type=MESH,
        )

    def drain(ref, sem):
        pltpu.make_async_copy(ref, ref, sem).wait()

    loads = [
        pltpu.make_async_copy(src, dst, win_sem.at[i])
        for i, (src, dst) in enumerate(
            (
                (k_hbm, k_ref),
                (v_hbm, v_ref),
                (wt_hbm, wt_ref),
                (q_hbm, q_ref),
                (ids_hbm, ids_ref),
                (gates_hbm, gates_ref),
                (res_hbm, res_ref),
                (win_hbm, win),
                (wout_hbm, wout),
            )
        )
    ]
    for load in loads:
        load.start()
    barrier = pltpu.get_barrier_semaphore()

    def far_first(i, size):
        return size // 2 + (1 - 2 * lax.rem(i, 2)) * (i // 2) + size

    def greet(dev):
        pl.semaphore_signal(barrier, inc=1, device_id={"seq": dev}, device_id_type=MESH)

    def greet_row(i, _):
        greet(y * row + lax.rem(at_row + far_first(i, row), row))
        return 0

    def greet_column(i, _):
        greet(seq(lax.rem(y + far_first(i // 2, ny), ny), z, lax.rem(c + i, 2)))
        return 0

    sib = seq(y, z, 1 - c)
    lax.fori_loop(1, row, greet_row, 0)
    lax.fori_loop(2, 2 * ny, greet_column, 0)

    loads[2].wait()
    for part in range(4):
        w_loc[part] = wt_ref[:, part * quarter : (part + 1) * quarter]
    pl.semaphore_wait(barrier, row + 2 * ny - 3)

    pa, pb = 2 * c, 2 * c + 1

    def keep(part, sem):
        pltpu.make_async_copy(w_loc.at[part], w_all.at[part, y, z, c], sem).start()

    def along_z(i, _):
        to = lax.rem(at_row + far_first(i, row), row)
        part = 2 * lax.rem(to, 2)
        remote(
            w_loc.at[part], w_all.at[part, y, z, c], w1_send.at[0], w1_recv.at[0], y * row + to
        ).start()
        return 0

    def to_column(yy, cc):
        part = 2 * cc + 1
        remote(
            w_loc.at[part],
            w_all.at[part, y, z, c],
            w1_send.at[1],
            w1_recv.at[1],
            seq(yy, z, cc),
        ).start()

    def along_y(i, _):
        to_column(lax.rem(y + far_first(i // 2, ny), ny), lax.rem(c + i, 2))
        return 0

    keep(pa, w1_recv.at[0])
    keep(pb, w1_recv.at[1])
    lax.fori_loop(1, row, along_z, 0)
    lax.fori_loop(2, 2 * ny, along_y, 0)
    to_column(y, 1 - c)

    loads[0].wait()
    loads[1].wait()

    def state(p):
        kp = k_ref[:, pl.ds(pl.multiple_of(p * 2 * dk, 2 * dk), 2 * dk)]
        vp = v_ref[:, pl.ds(pl.multiple_of(p * 2 * dv, 2 * dv), 2 * dv)]
        kv = dot(kp, vp, ((0,), (0,)))
        s_loc[2 * p] = kv[:dk, :dv].astype(BF)
        s_loc[2 * p + 1] = kv[dk:, dv:].astype(BF)

    hh = heads // 2
    own, other = c * hh, (1 - c) * hh
    first_core = c == 0
    for p in range(hh // 2):
        state(other // 2 + p)
    remote(s_loc.at[pl.ds(other, hh)], s_sib, s0_send, s0_recv, sib).start()
    for p in range(hh // 2):
        state(own // 2 + p)

    def tell(cc, yy):
        pl.semaphore_signal(
            met, inc=1, device_id={"seq": seq(yy, z, cc)}, device_id_type=MESH
        )

    def tell_column(i, _):
        tell(c, lax.rem(y + i, ny))
        return 0

    lax.fori_loop(1, ny, tell_column, 0)

    eye = lax.broadcasted_iota(jnp.int32, (length, length), 0) == lax.broadcasted_iota(
        jnp.int32, (length, length), 1
    )
    below = lax.broadcasted_iota(jnp.int32, (length, length), 1) < lax.broadcasted_iota(
        jnp.int32, (length, length), 0
    )
    above = lax.broadcasted_iota(jnp.int32, (length, length), 0) < lax.broadcasted_iota(
        jnp.int32, (length, length), 1
    )

    for load in loads[4:7]:
        load.wait()

    def column(r):
        return jnp.sum(jnp.where(eye, r, 0.0), axis=1, keepdims=True)

    def turn_of(e):
        dy = ((e >> (row.bit_length() - 1)) + (ny - y)) & (ny - 1)
        dz = ((e >> 1) + (nz - z)) & (nz - 1)
        dc = (e + c) & 1
        return ((dy * row + dz * 2 + dc) * 45) & (n - 1)

    id_row = [turn_of(ids_ref[j : j + 1, :]).astype(F32) for j in range(TOP)]
    id_col = [column(r) for r in id_row]
    gate_col = [column(gates_ref[j : j + 1, :]) for j in range(TOP)]
    place_row, place_col = [], []
    for j in range(TOP):
        row_count, col_count = 0.0, 0.0
        for i in range(TOP):
            row_count = row_count + jnp.where(above & (id_col[i] == id_row[j]), 1.0, 0.0)
            col_count = col_count + jnp.where(below & (id_col[j] == id_row[i]), 1.0, 0.0)
        place_row.append(id_row[j] * CAP + jnp.sum(row_count, axis=0, keepdims=True))
        place_col.append(id_col[j] * CAP + jnp.sum(col_count, axis=1, keepdims=True))
    rows = n * CAP
    r_iota = lax.broadcasted_iota(jnp.int32, (rows, length), 0).astype(F32)
    spread[...] = jnp.where(
        (r_iota == place_row[0]) | (r_iota == place_row[1]), 1.0, 0.0
    ).astype(BF)

    drain(s_sib, s0_recv)
    for i in range(hh):
        both = s_loc[own + i].astype(F32) + s_sib[i].astype(F32)
        s_pair[i] = both.astype(BF)
    pltpu.make_async_copy(s_pair.at[z], r1.at[z], s1_recv).start()

    def phase1(i, _):
        to = lax.rem(z + far_first(i, nz), nz)
        remote(s_pair.at[to], r1.at[z], s1_send, s1_recv, seq(y, to, c)).start()
        return 0

    lax.fori_loop(1, nz, phase1, 0)

    t_row = lax.broadcasted_iota(jnp.int32, (2 * length, length), 0)
    t_col = lax.broadcasted_iota(jnp.int32, (2 * length, length), 1)
    causal = lax.rem(t_row, length) >= t_col
    first = lax.broadcasted_iota(jnp.int32, (length, 2 * dk), 1) < dk

    def two_heads(p):
        qp = q_ref[:, pl.ds(pl.multiple_of(p * 2 * dk, 2 * dk), 2 * dk)]
        zero = jnp.zeros_like(qp)
        return jnp.concatenate(
            [jnp.where(first, qp, zero), jnp.where(first, zero, qp)], axis=0
        )

    def inside(p, _):
        kp = k_ref[:, pl.ds(pl.multiple_of(p * 2 * dk, 2 * dk), 2 * dk)]
        at = pl.multiple_of(p * 2 * dv, 2 * dv)
        scores = dot(two_heads(p), kp, ((1,), (1,)))
        scores = jnp.where(causal, scores, 0.0).astype(BF)
        vp = v_ref[:, pl.ds(at, 2 * dv)]
        intra[:, pl.ds(at, dv)] = dot(scores[:length], vp[:, :dv])
        intra[:, pl.ds(pl.multiple_of(at + dv, dv), dv)] = dot(scores[length:], vp[:, dv:])
        return 0

    loads[3].wait()
    half = heads // 4
    lax.fori_loop(0, half, inside, 0)

    def mod_y(v):
        return lax.rem(v + 2 * ny, ny)

    def mod_z(v):
        return lax.rem(v + 2 * nz, nz)

    def piece(axis, origin, h, many=1):
        if axis == 0:
            return w_all.at[pa, origin, pl.ds(h * (nz // cut), many * (nz // cut))]
        return w_all.at[pb, pl.ds(h * (ny // cut), many * (ny // cut)), origin]

    def pieces(axis, way, step):
        size = ny if axis == 0 else nz
        mine = tuple(range(way * cut // 2, (way + 1) * cut // 2))
        if 2 * step > size:
            return ()
        return mine if 2 * step == size else mine + tuple(set(range(cut)) - set(mine))

    def to_sibling(ref):
        remote(ref, ref, sib_send, sib_recv, sib).start()

    def ring_copy(axis, way, step, h):
        mod, at = (mod_y, y) if axis == 0 else (mod_z, z)
        sign = 1 if way == 0 else -1
        ref = piece(axis, mod(at - sign * (step - 1)), h)
        dev = seq(mod(at + sign), z, c) if axis == 0 else seq(y, mod(at + sign), c)
        place = (axis, way, step - 1, h)
        return remote(ref, ref, ring_send.at[place], ring_recv.at[place], dev)

    def ring_step(step):
        for turn in range(cut):
            for axis in (0, 1):
                mod, at = (mod_y, y) if axis == 0 else (mod_z, z)
                for way in (0, 1):
                    order = pieces(axis, way, step)
                    if turn < len(order):
                        h = order[turn]
                        origin = mod(at - step if way == 0 else at + step)
                        drain(piece(axis, origin, h), ring_recv.at[axis, way, step - 1, h])
                        if h in pieces(axis, way, step + 1):
                            ring_copy(axis, way, step + 1, h).start()
                        if turn == len(order) - 1:
                            to_sibling(piece(axis, origin, min(order), len(order)))

    def ring_open(axis):
        for turn in range(cut):
            for way in (0, 1):
                if turn < len(pieces(axis, way, 1)):
                    ring_copy(axis, way, 1, pieces(axis, way, 1)[turn]).start()

    drain(w_all.at[pa, y], w1_recv.at[0])
    ring_open(0)
    drain(w_all.at[pb, :, z], w1_recv.at[1])
    ring_open(1)
    to_sibling(w_all.at[pa, y])
    to_sibling(w_all.at[pb, :, z])

    lax.fori_loop(half, heads // 2, inside, 0)

    drain(r1, s1_recv)
    total = r1[0].astype(F32)
    for i in range(1, nz):
        total = total + r1[i].astype(F32)
    tot[...] = total.astype(BF)
    pltpu.make_async_copy(tot, r2.at[y], s2_recv).start()

    def phase2(i, _):
        yy = lax.rem(y + far_first(i, ny), ny)
        remote(tot, r2.at[y], s2_send, s2_recv, seq(yy, z, c)).start()
        return 0

    lax.fori_loop(1, ny, phase2, 0)

    ring_step(1)

    drain(r2, s2_recv)
    run = jnp.zeros(total.shape, F32)
    for yy in range(ny):
        run = run + jnp.where(yy < y, r2[yy].astype(F32), 0.0)
    for i in range(nz):
        p_out[i] = run.astype(BF)
        if i < nz - 1:
            run = run + r1[i].astype(F32)
    pltpu.make_async_copy(p_out.at[z], r3.at[z], s3_recv).start()

    def phase3(i, _):
        to = lax.rem(z + far_first(i, nz), nz)
        remote(p_out.at[to], r3.at[z], s3_send, s3_recv, seq(y, to, c)).start()
        return 0

    lax.fori_loop(1, nz, phase3, 0)

    ring_step(2)

    drain(r3, s3_recv)
    for i in range(hh):
        chip = r3[i].astype(F32)
        theirs = chip + jnp.where(first_core, s_loc[own + i].astype(F32), 0.0)
        s_pair_out[i] = theirs.astype(BF)
    remote(s_pair_out, prefix.at[pl.ds(own, hh)], s4_send, s4_recv, sib).start()
    for i in range(hh):
        chip = r3[i].astype(F32)
        mine = chip + jnp.where(first_core, 0.0, s_sib[i].astype(F32))
        prefix[own + i] = mine.astype(BF)

    ring_step(3)

    position = me * length + lax.broadcasted_iota(jnp.int32, (length, 1), 0)
    scaling = lax.rsqrt((position.astype(F32) + 1.0) * dk)

    def before(p):
        past = prefix[pl.ds(2 * p, 2)].reshape(2 * dk, dv)
        earlier = dot(two_heads(p), past)
        for h in range(2):
            cols = pl.ds(pl.multiple_of((2 * p + h) * dv, dv), dv)
            attended[:, cols] = (
                (intra[:, cols] + earlier[h * length : (h + 1) * length]) * scaling
            ).astype(BF)

    for p in range(hh // 2):
        before(own // 2 + p)
    drain(prefix.at[pl.ds(other, hh)], s4_recv)
    for p in range(hh // 2):
        before(other // 2 + p)

    for step in range(4, max(ny, nz) // 2 + 1):
        ring_step(step)

    def project(part):
        cols = pl.ds(pl.multiple_of(part * quarter, quarter), quarter)
        return dot(attended[:, cols], w_all[part].reshape(width, quarter), ((1,), (1,)))

    projected = project(pa) + project(pb)
    drain(w_all.at[pl.ds(2 * (1 - c), 2)], sib_recv)
    projected = projected + (project(2 * (1 - c)) + project(2 * (1 - c) + 1))
    hidden = (res_ref[...].astype(F32) + projected).astype(BF)
    hidden_float = hidden.astype(F32)
    intra[:, :width] = hidden_float
    normed = (
        hidden_float
        * lax.rsqrt(jnp.mean(hidden_float * hidden_float, axis=-1, keepdims=True) + 1e-06)
    ).astype(BF)

    def offset(i):
        j = lax.rem(i * 37, n)
        return j // row, lax.rem(j // 2, nz), lax.rem(j, 2)

    def ahead(i):
        dy, dz, dc = offset(i)
        return seq(lax.rem(y + dy, ny), lax.rem(z + dz, nz), lax.rem(c + dc, 2))

    def behind(i):
        dy, dz, dc = offset(i)
        return seq(lax.rem(y - dy + ny, ny), lax.rem(z - dz + nz, nz), lax.rem(c - dc + 2, 2))

    per = n // GROUPS
    pl.semaphore_wait(met, ny - 1)

    def fill(g):
        mine = spread[pl.ds(pl.multiple_of(g * per * CAP, per * CAP), per * CAP)]
        xb[pl.ds(g * per, per)] = dot(mine, normed).astype(BF).reshape(per, CAP, width)

    def dispatch(i, _):
        remote(xb.at[i], xr.at[i], x_send, x_recv.at[i // per], ahead(i)).start()
        return 0

    fill(0)
    pltpu.make_async_copy(xb.at[0], xr.at[0], x_recv.at[0]).start()
    lax.fori_loop(1, per, dispatch, 0)
    for g in range(1, GROUPS):
        fill(g)
        lax.fori_loop(g * per, (g + 1) * per, dispatch, 0)

    loads[7].wait()
    loads[8].wait()

    def expert(g):
        lo = g * per
        drain(xr.at[pl.ds(lo, per)], x_recv.at[g])
        x = xr[pl.ds(lo, per)].reshape(per * CAP, width)
        act = dot(x, win[...])
        gate, up = act[:, :he], act[:, he:]
        inner = (gate / (1.0 + jnp.exp(-gate)) * up).astype(BF)
        yb[pl.ds(lo, per)] = dot(inner, wout[...]).astype(BF).reshape(per, CAP, width)

    def give_back(i, _):
        to = behind(i)
        remote(yb.at[i], ret.at[i], y_send, y_recv.at[i // per], to).start()
        return 0

    expert(0)
    pltpu.make_async_copy(yb.at[0], ret.at[0], y_recv.at[0]).start()
    lax.fori_loop(1, per, give_back, 0)

    def group(g, _):
        expert(g)
        lax.fori_loop(g * per, (g + 1) * per, give_back, 0)
        return 0

    lax.fori_loop(1, GROUPS, group, 0)

    wide = per * CAP
    r_lane = lax.broadcasted_iota(jnp.int32, (length, wide), 1).astype(F32)
    combined = jnp.zeros((length, width), F32)
    for g in range(GROUPS):
        picks = jnp.concatenate(
            [
                jnp.where(r_lane + g * wide == place_col[j], 1.0, 0.0).astype(BF)
                for j in range(TOP)
            ],
            axis=0,
        )
        drain(ret.at[pl.ds(g * per, per)], y_recv.at[g])
        picked = dot(picks, ret[g * per : (g + 1) * per].reshape(wide, width))
        combined = combined + (picked[:length] * gate_col[0] + picked[length:] * gate_col[1])
    o_ref[...] = (intra[:, :width] + combined).astype(BF)

    drain(s_sib, s0_send)
    drain(r1.at[pl.ds(0, nz - 1)], s1_send)
    drain(r2.at[pl.ds(0, ny - 1)], s2_send)
    drain(r3.at[pl.ds(0, nz - 1)], s3_send)
    drain(s_sib, s4_send)
    drain(w_all.at[0, 0, pl.ds(0, nz - 1)], w1_send.at[0])
    drain(w_loc.at[0], w1_send.at[0])
    drain(w_all.at[0, pl.ds(0, ny - 1), 0], w1_send.at[1])
    drain(w_loc.at[0], w1_send.at[1])
    for axis in (0, 1):
        for step in range(1, max(ny, nz) // 2 + 1):
            for way in (0, 1):
                for h in pieces(axis, way, step):
                    ring_copy(axis, way, step, h).wait_send()
    drain(w_all.at[pl.ds(2 * c, 2)], sib_send)
    drain(xb.at[pl.ds(0, n - 1)], x_send)
    drain(yb.at[pl.ds(0, n - 1)], y_send)


def layer(ny, nz, heads, dk, dv, q, k, v, res, wt, w_in, w_out, ids, gates):
    n = ny * nz * 2
    length, width = res.shape
    cols = wt.shape[0]
    quarter = heads * dv // 4
    vmem = pl.BlockSpec(memory_space=pltpu.VMEM)
    hbm = pl.BlockSpec(memory_space=pl.ANY)
    steps = max(ny, nz) // 2
    dma = pltpu.SemaphoreType.DMA
    rows = (n, CAP, width)
    return pl.pallas_call(
        functools.partial(layer_kernel, ny, nz, heads, dk, dv),
        out_shape=pltpu.VMEM((length, width), BF),
        in_specs=[hbm] * 9,
        out_specs=vmem,
        scratch_shapes=[
            *[pltpu.VMEM(a.shape, a.dtype) for a in (q, k, v, res, wt, ids, gates)],
            pltpu.VMEM((heads, dk, dv), BF),
            pltpu.VMEM((nz, dk, dv), BF),
            pltpu.VMEM((nz, dk, dv), BF),
            pltpu.VMEM((nz, dk, dv), BF),
            pltpu.VMEM((dk, dv), BF),
            pltpu.VMEM((nz, dk, dv), BF),
            pltpu.VMEM((nz, dk, dv), BF),
            pltpu.VMEM((ny, dk, dv), BF),
            pltpu.VMEM((nz, dk, dv), BF),
            pltpu.VMEM((heads, dk, dv), BF),
            pltpu.VMEM((4, cols, quarter), BF),
            pltpu.VMEM((4, ny, nz, 2, cols, quarter), BF),
            pltpu.VMEM((length, heads * dv), F32),
            pltpu.VMEM((length, heads * dv), BF),
            pltpu.VMEM(w_in.shape, BF),
            pltpu.VMEM(w_out.shape, BF),
            pltpu.VMEM((n * CAP, length), BF),
            pltpu.VMEM(rows, BF),
            pltpu.VMEM(rows, BF),
            pltpu.VMEM(rows, BF),
            pltpu.VMEM(rows, BF),
            *[dma] * 10,
            dma((2,)),
            dma((2,)),
            pltpu.SemaphoreType.REGULAR,
            dma((2, 2, steps, 4)),
            dma((2, 2, steps, 4)),
            dma,
            dma,
            dma,
            dma((GROUPS,)),
            dma,
            dma((GROUPS,)),
            dma((9,)),
        ],
        compiler_params=pltpu.CompilerParams(
            collective_id=0, has_side_effects=True, vmem_limit_bytes=60 * 2**20
        ),
        name="layer",
    )(q, k, v, res, wt, w_in, w_out, ids, gates)


def solution(mesh, ny=8, nz=8, heads=16, dk=64, dv=128):
    def per_device(q, k, v, res, w, w_in, w_out, ids, gates):
        return layer(
            ny, nz, heads, dk, dv, q, k, v, res, w.T, w_in[0], w_out[0], ids.T, gates.T
        )

    tokens = P(("win", "seq"), None)
    experts = P("seq", None, None)
    return jax.shard_map(
        per_device,
        mesh=mesh,
        in_specs=(tokens,) * 4 + (P(None, "seq"), experts, experts, tokens, tokens),
        out_specs=tokens,
        check_vma=False,
    )
```
